512 devices in a mesh: head: 16 (over z_hi, x, core), seq: 32 (over y, z_lo).
Axes of the slice: x: 4, y: 4, z: 16 (z_hi: 2, z_lo: 8; z = z_hi * 8 + z_lo), core: 2. Of those that a mesh axis runs over, the one named last changes fastest.
Arguments:
- queries: bfloat16 [1536, 8192], P('seq', 'head'), may hold values from -2.5 to 2.5
- keys: bfloat16 [1024, 20480], P('head', 'seq'), may hold values from -2.5 to 2.5
- values: bfloat16 [1024, 20480], P('head', 'seq'), may hold values from -6 to 6
- outputs: bfloat16 [1536, 8192], P('seq', 'head'), may hold values from -6 to 6
- out_grad: bfloat16 [1536, 8192], P('seq', 'head'), may hold values from -192 to 192
- logsumexp: float32 [1536, 64], P('seq', 'head'), may hold values from 8.5 to 9.5
Outputs:
- query_grad: bfloat16 [1536, 8192], P('seq', 'head')
- key_grad: bfloat16 [1024, 20480], P('head', 'seq')
- value_grad: bfloat16 [1024, 20480], P('head', 'seq')
The draws below stay inside these ranges and needn't reach their ends.
All inputs are finite; a program needn't handle non-finite values.
Results may differ from the reference program's by a relative error of at most 0.005.
Values may be sent and summed in bfloat16 or wider, within the bound.
No kernel may reach another device: no remote copies, remote signals or barrier semaphores. Data moves between devices by JAX's collectives and lax.ppermute only.
A program may use at most 64 MiB of HBM per device.

```python
import jax
import jax.numpy as jnp
from jax import lax

DH = 128
GROUP = 8
HEADS = 64
KVH = 8
TXT = 1536
VIS = 20480


def block_scale(rng, dims, cuts, low, top_value):
    level, own = 1.0, jax.random.fold_in(rng, 6)
    for dim, shards_of in cuts:
        steps = jnp.exp(jax.random.uniform(jax.random.fold_in(own, dim), (shards_of,), jnp.float32, low / len(cuts), top_value / len(cuts)))
        level = level * jnp.repeat(steps, dims[dim] // shards_of).reshape([-1 if axis == dim else 1 for axis in range(len(dims))])
    return level


def gaussian(key, shape, scale, most, pieces=(), dtype=jnp.bfloat16):
    values = jax.random.normal(key, shape, jnp.float32) * scale
    if len(pieces) > 0:
        values = block_scale(key, shape, pieces, -0.22, 0.18) * values
    return jnp.clip(values, min=-most, max=most).astype(dtype)


def setup_inputs(seed: int = 0) -> dict:
    seeds = jax.random.split(jax.random.key(seed), 7)
    queries = gaussian(seeds[0], (TXT, HEADS * DH), 1.0, 2.5, ((0, 32), (1, 16)))
    keys = gaussian(seeds[1], (KVH * DH, VIS), 1.0, 2.5, ((0, 16), (1, 32)))
    values = gaussian(seeds[2], (KVH * DH, VIS), 1.0, 6.0, ((0, 16), (1, 32)))
    outputs = gaussian(seeds[3], (TXT, HEADS * DH), 1.0, 6.0, ((0, 32), (1, 16)))
    out_grad = gaussian(seeds[4], (TXT, HEADS * DH), 32.0, 192.0, ((0, 32), (1, 16)))
    logsumexp = jnp.clip(8.5 + 1.0 * jax.random.uniform(seeds[5], (TXT, HEADS), jnp.float32) ** block_scale(seeds[5], (TXT, HEADS), ((0, 32), (1, 16)), -0.2, 0.2), 8.5, 9.5)
    return dict(queries=queries, keys=keys, values=values, outputs=outputs, out_grad=out_grad, logsumexp=logsumexp)


def head_grads(key_head, value_head, query_head, grad_head, lse_head, dterm_head, softmax_scale):
    scores = jnp.dot(query_head, key_head.T, preferred_element_type=jnp.float32) * softmax_scale
    probs = jnp.exp(scores - lse_head[:, None])
    dprobs = jnp.dot(grad_head, value_head.T, preferred_element_type=jnp.float32)
    dscores = (probs * (dprobs - dterm_head[:, None])).astype(jnp.bfloat16)
    probs_low = probs.astype(jnp.bfloat16)
    dv_term = jnp.dot(probs_low.T, grad_head, preferred_element_type=jnp.float32)
    dk_term = jnp.dot(dscores.T, query_head, preferred_element_type=jnp.float32) * softmax_scale
    dq_head = jnp.dot(dscores, key_head, preferred_element_type=jnp.float32) * softmax_scale
    return dq_head, dk_term, dv_term


def reference(queries, keys, values, outputs, out_grad, logsumexp):
    softmax_scale = DH ** -0.5
    q_heads = queries.reshape(TXT, HEADS, DH).transpose(1, 0, 2).reshape(KVH, GROUP, TXT, DH)
    g_heads = out_grad.reshape(TXT, HEADS, DH).transpose(1, 0, 2).reshape(KVH, GROUP, TXT, DH)
    dterm = jnp.sum((out_grad.astype(jnp.float32) * outputs.astype(jnp.float32)).reshape(TXT, HEADS, DH), axis=2)
    dterm_heads = dterm.T.reshape(KVH, GROUP, TXT)
    lse_heads = logsumexp.T.reshape(KVH, GROUP, TXT)
    k_heads = keys.reshape(KVH, DH, VIS).transpose(0, 2, 1)
    v_heads = values.reshape(KVH, DH, VIS).transpose(0, 2, 1)

    def per_group(packed):
        key_head, value_head, q_group, g_group, lse_group, dterm_group = packed

        def per_head(state_pair, inner):
            query_head, grad_head, lse_head, dterm_head = inner
            dq_head, dk_term, dv_term = head_grads(key_head, value_head, query_head, grad_head, lse_head, dterm_head, softmax_scale)
            return (state_pair[0] + dk_term, state_pair[1] + dv_term), dq_head

        zero_kv = jnp.zeros((VIS, DH), jnp.float32)
        (dk_sum, dv_sum), dq_group = lax.scan(per_head, (zero_kv, zero_kv), (q_group, g_group, lse_group, dterm_group))
        return dq_group, dk_sum, dv_sum

    dq_all, dk_all, dv_all = lax.map(per_group, (k_heads, v_heads, q_heads, g_heads, lse_heads, dterm_heads))
    query_grad = dq_all.reshape(HEADS, TXT, DH).transpose(1, 0, 2).reshape(TXT, HEADS * DH).astype(jnp.bfloat16)
    key_grad = dk_all.transpose(0, 2, 1).reshape(KVH * DH, VIS).astype(jnp.bfloat16)
    value_grad = dv_all.transpose(0, 2, 1).reshape(KVH * DH, VIS).astype(jnp.bfloat16)
    return query_grad, key_grad, value_grad
```

```python
import jax
import jax.numpy as jnp
from jax import lax
from jax.experimental import pallas as pl
from jax.experimental.pallas import tpu as pltpu
from jax.sharding import Mesh, PartitionSpec as P

DH = 128
HQ = 4
WIDTH = HQ * DH
SCALE = DH**-0.5
LOG2E = 1.4426950408889634
BF = jnp.bfloat16
F32 = jnp.float32


def pieces(value):
    out = []
    for _ in range(3):
        part = lax.reduce_precision(value, 8, 7)
        out.append(part.astype(BF))
        value = value - part
    return out


def grads_kernel(x_ref, k_ref, v_ref, dq_ref, dk_ref, dv_ref):
    chunks, _, cols = k_ref.shape
    rows = x_ref.shape[0]
    first = pl.program_id(0) == 0

    @pl.when(first)
    def _():
        dk_ref[...] = jnp.zeros_like(dk_ref)
        dv_ref[...] = jnp.zeros_like(dv_ref)

    lane = lax.broadcasted_iota(jnp.int32, (rows, DH), 1)
    row = lax.broadcasted_iota(jnp.int32, (DH, cols), 0)
    k_ones = jnp.where((row < 6 * HQ) & (lax.rem(row, 6) < 3), 1.0, 0.0).astype(BF)
    v_ones = jnp.where((row < 6 * HQ) & (lax.rem(row, 6) >= 3), 1.0, 0.0).astype(BF)
    stats = x_ref[:, 2 * WIDTH : 2 * WIDTH + DH]
    for h in range(HQ):
        q_h = x_ref[:, h * DH : (h + 1) * DH]
        g_h = x_ref[:, WIDTH + h * DH : WIDTH + (h + 1) * DH]
        s_h = jnp.where((lane >= 6 * h) & (lane < 6 * h + 6), stats, jnp.zeros_like(stats))
        q_s = jnp.concatenate([q_h, s_h], 1)
        g_s = jnp.concatenate([g_h, s_h], 1)
        dq = jnp.zeros((rows, DH), F32)
        for j in range(chunks):
            k_j = k_ref[j]
            v_j = v_ref[j]
            s = jnp.dot(q_s, jnp.concatenate([k_j, k_ones], 0), preferred_element_type=F32)
            p = jnp.exp2(s * (SCALE * LOG2E))
            dp = jnp.dot(g_s, jnp.concatenate([v_j, v_ones], 0), preferred_element_type=F32)
            ds = (p * dp).astype(BF)
            pb = p.astype(BF)
            over_rows = (((0,), (0,)), ((), ()))
            dv_ref[j] += lax.dot_general(g_h, pb, over_rows, preferred_element_type=F32)
            dk_ref[j] += lax.dot_general(q_h, ds, over_rows, preferred_element_type=F32)
            dq += lax.dot_general(ds, k_j, (((1,), (1,)), ((), ())), preferred_element_type=F32)
        dq_ref[:, h * DH : (h + 1) * DH] = (dq * SCALE).astype(BF)


def grads(x, k_all, v_all, block):
    rows, width = x.shape
    kv_shape = k_all.shape
    kv_spec = pl.BlockSpec(kv_shape, lambda i: (0, 0, 0))
    work = rows * HQ * kv_shape[0] * kv_shape[2]
    return pl.pallas_call(
        grads_kernel,
        grid=(rows // block,),
        in_specs=[pl.BlockSpec((block, width), lambda i: (i, 0)), kv_spec, kv_spec],
        out_specs=[pl.BlockSpec((block, WIDTH), lambda i: (i, 0)), kv_spec, kv_spec],
        out_shape=[
            jax.ShapeDtypeStruct((rows, WIDTH), BF),
            jax.ShapeDtypeStruct(kv_shape, F32),
            jax.ShapeDtypeStruct(kv_shape, F32),
        ],
        compiler_params=pltpu.CompilerParams(vmem_limit_bytes=48 << 20),
        cost_estimate=pl.CostEstimate(flops=10 * work * DH, bytes_accessed=8 << 20, transcendentals=work),
        name="grads",
    )(x, k_all, v_all)


def per_device(queries, keys, values, outputs, out_grad, logsumexp):
    rows = queries.shape[0]
    half, cols = keys.shape
    zn = lax.axis_size("zl")
    yn = lax.axis_size("y")
    core = lax.axis_index("core")
    swap = [(0, 1), (1, 0)]

    dterm = jnp.sum(
        (out_grad.astype(F32) * outputs.astype(F32)).reshape(rows, HQ, DH), axis=2
    )
    stats = jnp.stack(pieces(logsumexp * (-1.0 / SCALE)) + pieces(-dterm), axis=2)
    stats = jnp.pad(stats.reshape(rows, 6 * HQ), ((0, 0), (0, DH - 6 * HQ)))
    x = jnp.concatenate([queries, out_grad, stats], 1)

    x_all = lax.all_to_all(jnp.broadcast_to(x, (zn,) + x.shape), "zl", 0, 0)
    x_all = x_all.reshape(zn * rows, x.shape[1])

    kv = jnp.stack([keys, values])
    kv_own = lax.all_gather(kv, "y")
    kv_other = lax.ppermute(kv_own, "core", swap)
    low = jnp.where(core == 0, kv_own, kv_other)
    high = jnp.where(core == 0, kv_other, kv_own)
    k_all = jnp.concatenate([low[:, 0], high[:, 0]], 1)
    v_all = jnp.concatenate([low[:, 1], high[:, 1]], 1)

    dq, dk, dv = grads(x_all, k_all, v_all, zn * rows // 2)

    dq = lax.all_to_all(dq.reshape(zn, rows, WIDTH), "zl", 0, 0)
    query_grad = jnp.sum(dq.astype(F32), axis=0).astype(BF)

    dkv = jnp.stack([dk * SCALE, dv], 1).reshape(yn, 2, 2, half, cols)
    keep = jnp.where(core == 0, dkv[:, :, 0], dkv[:, :, 1])
    send = jnp.where(core == 0, dkv[:, :, 1], dkv[:, :, 0]).astype(BF)
    both = keep + lax.ppermute(send, "core", swap).astype(F32)
    parts = lax.all_to_all(both.astype(BF), "y", 0, 0)
    total = jnp.sum(parts.astype(F32), axis=0).astype(BF)
    return query_grad, total[0], total[1]


def solution(mesh):
    devices = mesh.devices.reshape(2, 4, 2, 4, 8)
    inner = Mesh(devices, ("zh", "x", "core", "y", "zl"))
    head = ("zh", "x", "core")
    seq = ("y", "zl")
    text = P(seq, head)
    visual = P(head, seq)
    return jax.shard_map(
        per_device,
        mesh=inner,
        in_specs=(text, visual, visual, text, text, text),
        out_specs=(text, visual, visual),
        check_vma=False,
    )
```

```python
import jax
import jax.numpy as jnp
from jax import lax
from jax.experimental import pallas as pl
from jax.experimental.pallas import tpu as pltpu
from jax.sharding import Mesh, PartitionSpec as P

DH = 128
HQ = 4
WIDTH = HQ * DH
SCALE = DH**-0.5
LOG2E = 1.4426950408889634
BF = jnp.bfloat16
F32 = jnp.float32
SWAP = [(0, 1), (1, 0)]
VMEM_GRADS = 60 << 20
MEDIUM = pltpu.CompilerParams(vmem_limit_bytes=12 << 20)
SMALL = pltpu.CompilerParams(vmem_limit_bytes=4 << 20)


def half_swap(value, core):
    rolled = jnp.concatenate([value[:, DH // 2 :], value[:, : DH // 2]], 1)
    return jnp.where(core == 0, value, rolled)


def prep_kernel(core_ref, q_ref, g_ref, o_ref, lse_ref, k_ref, v_ref, x_ref, kv_ref):
    core = core_ref[0]
    rows = q_ref.shape[0]
    lane = lax.broadcasted_iota(jnp.int32, (rows, DH), 1)
    lse = jnp.transpose(lse_ref[...]) * (-1.0 / SCALE)
    stats = jnp.zeros((rows, DH), F32)
    for h in range(HQ):
        at = pl.ds(h * DH, DH)
        q = q_ref[:, at].astype(F32)
        g = g_ref[:, at].astype(F32)
        dterm = jnp.sum(g * o_ref[:, at].astype(F32), axis=1, keepdims=True)
        mine = (lane & (HQ - 1)) == h
        stats = jnp.where(mine & (lane < 3 * HQ), lse[:, h : h + 1], stats)
        stats = jnp.where(mine & (lane >= 3 * HQ) & (lane < 6 * HQ), -dterm, stats)
        x_ref[:, at] = half_swap(q, core).astype(BF)
        x_ref[:, pl.ds(WIDTH + h * DH, DH)] = half_swap(g, core).astype(BF)
    high = stats.astype(BF).astype(F32)
    rest = stats - high
    middle = rest.astype(BF).astype(F32)
    group = lax.shift_right_logical(lane, 2)
    first = (group == 0) | (group == 3)
    second = (group == 1) | (group == 4)
    stats = jnp.where(first, high, jnp.where(second, middle, rest - middle))
    x_ref[:, pl.ds(2 * WIDTH, DH)] = stats.astype(BF)
    kv_ref[0] = k_ref[...]
    kv_ref[1] = v_ref[...]


def prep(core, queries, out_grad, outputs, lse_t, keys, values):
    rows = queries.shape[0]
    return pl.pallas_call(
        prep_kernel,
        in_specs=[pl.BlockSpec(memory_space=pltpu.SMEM)] + [pl.BlockSpec(memory_space=pltpu.VMEM)] * 6,
        out_shape=[
            jax.ShapeDtypeStruct((rows, 2 * WIDTH + DH), BF),
            jax.ShapeDtypeStruct((2,) + keys.shape, BF),
        ],
        name="prep",
    )(core, queries, out_grad, outputs, lse_t, keys, values)


def grads_kernel(last, *refs):
    if last:
        x_ref, own_ref, other_ref, keep_in, send_in, dq_ref, keep_ref, send_ref, q_s, g_s, acc = refs
    else:
        x_ref, own_ref, other_ref, dq_ref, keep_ref, send_ref, q_s, g_s, acc = refs
    blocks, rows, _ = x_ref.shape
    half, cols = own_ref.shape[2:]
    step = pl.program_id(0)

    @pl.when(step == 0)
    def _():
        lane = lax.broadcasted_iota(jnp.int32, (rows, DH), 1)
        for b in range(blocks):
            stats = x_ref[b, :, 2 * WIDTH : 2 * WIDTH + DH].astype(F32)
            for h in range(HQ):
                to = pl.ds((h * blocks + b) * rows, rows)
                mine = jnp.where((lane & (HQ - 1)) == h, stats, 0.0).astype(BF)
                q_s[to, :DH] = x_ref[b, :, h * DH : (h + 1) * DH]
                g_s[to, :DH] = x_ref[b, :, WIDTH + h * DH : WIDTH + (h + 1) * DH]
                q_s[to, DH:] = mine
                g_s[to, DH:] = mine

    row = lax.broadcasted_iota(jnp.int32, (DH, cols), 0)
    k_ones = jnp.where(row < 3 * HQ, 1.0, 0.0).astype(BF)
    v_ones = jnp.where((row >= 3 * HQ) & (row < 6 * HQ), 1.0, 0.0).astype(BF)
    k = jnp.concatenate([own_ref[0, 0], other_ref[0, 0]], 0)
    v = jnp.concatenate([own_ref[0, 1], other_ref[0, 1]], 0)
    s = jnp.dot(q_s[...], jnp.concatenate([k, k_ones], 0), preferred_element_type=F32)
    p = jnp.exp2(s * (SCALE * LOG2E))
    dp = jnp.dot(g_s[...], jnp.concatenate([v, v_ones], 0), preferred_element_type=F32)
    ds = (p * dp).astype(BF)
    pb = p.astype(BF)
    over_rows = (((0,), (0,)), ((), ()))
    dv = lax.dot_general(g_s[:, :DH], pb, over_rows, preferred_element_type=F32)
    dk = lax.dot_general(q_s[:, :DH], ds, over_rows, preferred_element_type=F32) * SCALE
    dq = lax.dot_general(ds, k, (((1,), (1,)), ((), ())), preferred_element_type=F32) * SCALE
    for i, part in enumerate((dk, dv)):
        keep = part[:half]
        send = part[half:]
        if last:
            keep = keep + keep_in[0, i]
            send = send + send_in[0, i]
        keep_ref[0, i] = keep
        send_ref[0, i] = send.astype(send_ref.dtype)

    @pl.when(step == 0)
    def _():
        acc[...] = dq

    @pl.when(step > 0)
    def _():
        acc[...] += dq

    @pl.when(step == pl.num_programs(0) - 1)
    def _():
        for b in range(blocks):
            for h in range(HQ):
                at = pl.ds((h * blocks + b) * rows, rows)
                dq_ref[b, :, h * DH : (h + 1) * DH] = acc[at, :].astype(BF)


def grads(x, own, other, before=None):
    blocks, rows, width = x.shape
    chunks, _, half, cols = own.shape
    total = blocks * rows * HQ
    last = before is not None
    kv_spec = pl.BlockSpec((1, 2, half, cols), lambda i: (i, 0, 0, 0))
    work = total * chunks * cols
    return pl.pallas_call(
        lambda *refs: grads_kernel(last, *refs),
        grid=(chunks,),
        in_specs=[pl.BlockSpec(x.shape, lambda i: (0, 0, 0)), kv_spec, kv_spec] + ([kv_spec] * 2 if last else []),
        out_specs=[pl.BlockSpec((blocks, rows, WIDTH), lambda i: (0, 0, 0)), kv_spec, kv_spec],
        out_shape=[
            jax.ShapeDtypeStruct((blocks, rows, WIDTH), BF),
            jax.ShapeDtypeStruct(own.shape, F32),
            jax.ShapeDtypeStruct(own.shape, BF if last else F32),
        ],
        scratch_shapes=[
            pltpu.VMEM((total, 2 * DH), BF),
            pltpu.VMEM((total, 2 * DH), BF),
            pltpu.VMEM((total, DH), F32),
        ],
        compiler_params=pltpu.CompilerParams(vmem_limit_bytes=VMEM_GRADS),
        cost_estimate=pl.CostEstimate(flops=10 * work * DH, bytes_accessed=4 << 20, transcendentals=work),
        name="grads",
    )(x, own, other, *(before or ()))


def sum_kernel(parts_ref, out_ref):
    total = parts_ref[0].astype(F32)
    for b in range(1, parts_ref.shape[0]):
        total = total + parts_ref[b].astype(F32)
    out_ref[...] = total.astype(out_ref.dtype)


def total_of(parts, dtype):
    return pl.pallas_call(
        sum_kernel,
        out_shape=jax.ShapeDtypeStruct(parts.shape[1:], dtype),
        compiler_params=SMALL,
        name="total_of",
    )(parts)


def query_kernel(core_ref, parts_ref, far_ref, out_ref):
    core = core_ref[0]
    for h in range(HQ):
        at = pl.ds(h * DH, DH)
        total = far_ref[:, at].astype(F32)
        for b in range(parts_ref.shape[0]):
            total = total + parts_ref[b, :, at].astype(F32)
        out_ref[:, at] = half_swap(total, core).astype(BF)


def query_total(core, parts, far):
    return pl.pallas_call(
        query_kernel,
        in_specs=[pl.BlockSpec(memory_space=pltpu.SMEM)] + [pl.BlockSpec(memory_space=pltpu.VMEM)] * 2,
        out_shape=jax.ShapeDtypeStruct(far.shape, BF),
        compiler_params=SMALL,
        name="query_total",
    )(core, parts, far)


def both_kernel(y_ref, keep_ref, got_ref, *out_refs):
    count = len(out_refs)
    for r, out_ref in enumerate(out_refs):
        at = lax.rem(y_ref[0] + r, count)
        out_ref[...] = (keep_ref[at] + got_ref[at].astype(F32)).astype(out_ref.dtype)


def both_cores(y, keep, got):
    one = keep.shape[1:]
    return pl.pallas_call(
        both_kernel,
        in_specs=[pl.BlockSpec(memory_space=pltpu.SMEM)] + [pl.BlockSpec(memory_space=pltpu.VMEM)] * 2,
        out_shape=[jax.ShapeDtypeStruct(one, BF) for r in range(keep.shape[0])],
        compiler_params=MEDIUM,
        name="both_cores",
    )(y, keep, got)


def visual_kernel(*refs):
    parts = refs[:-2]
    for i, out_ref in enumerate(refs[-2:]):
        total = parts[0][i].astype(F32)
        for part in parts[1:]:
            total = total + part[i].astype(F32)
        out_ref[...] = total.astype(BF)


def visual_total(parts):
    one = jax.ShapeDtypeStruct(parts[0].shape[1:], BF)
    return pl.pallas_call(
        visual_kernel, out_shape=[one, one], compiler_params=SMALL, name="visual_total"
    )(*parts)


def along_y(value, steps):
    count = lax.axis_size("y")
    return lax.ppermute(value, "y", [(i, (i + steps) % count) for i in range(count)])


def to_quad(block):
    count = lax.axis_size("zi")
    return lax.all_to_all(jnp.broadcast_to(block, (count,) + block.shape), "zi", 0, 0)


def per_device(queries, keys, values, outputs, out_grad, logsumexp):
    core = lax.axis_index("core").astype(jnp.int32).reshape(1)
    x, kv = prep(core, queries, out_grad, outputs, logsumexp.T, keys, values)

    far = lax.ppermute(x, "zq", SWAP)
    x_near = to_quad(x)

    own = lax.all_gather(kv, "y")
    far, own = lax.optimization_barrier((far, own))
    other = lax.ppermute(own, "core", SWAP)
    x_far = to_quad(far)

    dq_near, keep, send = grads(x_near, own, other)
    near = lax.all_to_all(dq_near, "zi", 0, 0)
    dq_far, keep, send = grads(x_far, own, other, (keep, send))
    near, dq_far = lax.optimization_barrier((near, dq_far))
    far_sum = total_of(lax.all_to_all(dq_far, "zi", 0, 0), BF)
    query_grad = query_total(core, near, lax.ppermute(far_sum, "zq", SWAP))

    y = lax.axis_index("y").astype(jnp.int32).reshape(1)
    both = both_cores(y, keep, lax.ppermute(send, "core", SWAP))
    parts = [both[0]] + [along_y(both[r], r) for r in range(1, len(both))]
    key_grad, value_grad = visual_total(parts)
    return query_grad, key_grad, value_grad


def solution(mesh):
    devices = mesh.devices.reshape(2, 4, 2, 4, 2, 4)
    inner = Mesh(devices, ("zh", "x", "core", "y", "zq", "zi"))
    head = ("zh", "x", "core")
    seq = ("y", "zq", "zi")
    text = P(seq, head)
    visual = P(head, seq)
    return jax.shard_map(
        per_device,
        mesh=inner,
        in_specs=(text, visual, visual, text, text, text),
        out_specs=(text, visual, visual),
        check_vma=False,
    )
```

```python
import jax
import jax.numpy as jnp
from jax import lax
from jax.experimental import pallas as pl
from jax.experimental.pallas import tpu as pltpu
from jax.sharding import Mesh, PartitionSpec as P

DH = 128
HQ = 4
WIDTH = HQ * DH
SCALE = DH**-0.5
LOG2E = 1.4426950408889634
BF = jnp.bfloat16
F32 = jnp.float32
SWAP = [(0, 1), (1, 0)]
VMEM_GRADS = 40 << 20
SPARE = 10
MEDIUM = pltpu.CompilerParams(vmem_limit_bytes=12 << 20)
SMALL = pltpu.CompilerParams(vmem_limit_bytes=4 << 20)


def half_swap(value, core):
    rolled = jnp.concatenate([value[:, DH // 2 :], value[:, : DH // 2]], 1)
    return jnp.where(core == 0, value, rolled)


def prep_kernel(core_ref, q_ref, g_ref, o_ref, lse_ref, k_ref, v_ref, x_ref, kv_ref):
    core = core_ref[0]
    rows = q_ref.shape[0]
    lane = lax.broadcasted_iota(jnp.int32, (rows, DH), 1)
    lse = jnp.transpose(lse_ref[...]) * (-1.0 / SCALE)
    stats = jnp.zeros((rows, DH), F32)
    for h in range(HQ):
        at = pl.ds(h * DH, DH)
        q = q_ref[:, at].astype(F32)
        g = g_ref[:, at].astype(F32)
        dterm = jnp.sum(g * o_ref[:, at].astype(F32), axis=1, keepdims=True)
        mine = (lane & (HQ - 1)) == h
        stats = jnp.where(mine & (lane < 3 * HQ), lse[:, h : h + 1], stats)
        stats = jnp.where(mine & (lane >= 3 * HQ) & (lane < 6 * HQ), -dterm, stats)
        x_ref[:, at] = half_swap(q, core).astype(BF)
        x_ref[:, pl.ds(WIDTH + h * DH, DH)] = half_swap(g, core).astype(BF)
    high = stats.astype(BF).astype(F32)
    rest = stats - high
    middle = rest.astype(BF).astype(F32)
    group = lax.shift_right_logical(lane, 2)
    first = (group == 0) | (group == 3)
    second = (group == 1) | (group == 4)
    stats = jnp.where(first, high, jnp.where(second, middle, rest - middle))
    x_ref[:, pl.ds(2 * WIDTH, DH)] = stats.astype(BF)
    kv_ref[0] = k_ref[...]
    kv_ref[1] = v_ref[...]


def prep(core, queries, out_grad, outputs, lse_t, keys, values):
    rows = queries.shape[0]
    return pl.pallas_call(
        prep_kernel,
        in_specs=[pl.BlockSpec(memory_space=pltpu.SMEM)] + [pl.BlockSpec(memory_space=pltpu.VMEM)] * 6,
        out_shape=[
            jax.ShapeDtypeStruct((rows, 2 * WIDTH + DH), BF),
            jax.ShapeDtypeStruct((2,) + keys.shape, BF),
        ],
        name="prep",
    )(core, queries, out_grad, outputs, lse_t, keys, values)


def grads_kernel(blocks, chunks, last, *refs):
    refs = list(refs)
    at_ref = refs.pop(0)
    if last:
        x_refs, refs = refs[:blocks], refs[blocks:]
    else:
        x_ref = refs.pop(0)
        x_refs = [x_ref.at[b] for b in range(blocks)]
    kv_refs, refs = refs[:chunks], refs[chunks:]
    if last:
        before_ref, dq_ref, keep_ref, send_ref, q_s, g_s, acc, held, kept, sems, out_sems = refs
        copies = [pltpu.make_async_copy(before_ref.at[j], held.at[j], sems.at[j]) for j in range(chunks)]
        for copy in copies:
            copy.start()
        out_copies = [pltpu.make_async_copy(kept.at[j], keep_ref.at[j], out_sems.at[j]) for j in range(chunks)]
    else:
        dq_ref, after_ref, q_s, g_s, acc, held, sems = refs
        copies = [pltpu.make_async_copy(held.at[j], after_ref.at[j], sems.at[j]) for j in range(chunks)]
    rows = x_refs[0].shape[0]
    _, _, half, cols = kv_refs[0].shape
    lane = lax.broadcasted_iota(jnp.int32, (rows, DH), 1)
    for b in range(blocks):
        stats = x_refs[b][:, 2 * WIDTH : 2 * WIDTH + DH].astype(F32)
        for h in range(HQ):
            to = pl.ds((h * blocks + b) * rows, rows)
            mine = jnp.where((lane & (HQ - 1)) == h, stats, 0.0).astype(BF)
            q_s[to, :DH] = x_refs[b][:, h * DH : (h + 1) * DH]
            g_s[to, :DH] = x_refs[b][:, WIDTH + h * DH : WIDTH + (h + 1) * DH]
            q_s[to, DH:] = mine
            g_s[to, DH:] = mine

    row = lax.broadcasted_iota(jnp.int32, (DH, cols), 0)
    k_ones = jnp.where(row < 3 * HQ, 1.0, 0.0).astype(BF)
    v_ones = jnp.where((row >= 3 * HQ) & (row < 6 * HQ), 1.0, 0.0).astype(BF)
    over_rows = (((0,), (0,)), ((), ()))
    for j in range(chunks):
        k = jnp.concatenate([kv_refs[j][0, 0], kv_refs[j][1, 0]], 0)
        v = jnp.concatenate([kv_refs[j][0, 1], kv_refs[j][1, 1]], 0)
        s = jnp.dot(q_s[...], jnp.concatenate([k, k_ones], 0), preferred_element_type=F32)
        p = jnp.exp2(s * (SCALE * LOG2E))
        dp = jnp.dot(g_s[...], jnp.concatenate([v, v_ones], 0), preferred_element_type=F32)
        ds = (p * dp).astype(BF)
        pb = p.astype(BF)
        dv = lax.dot_general(g_s[:, :DH], pb, over_rows, preferred_element_type=F32)
        dk = lax.dot_general(q_s[:, :DH], ds, over_rows, preferred_element_type=F32) * SCALE
        dq = lax.dot_general(ds, k, (((1,), (1,)), ((), ())), preferred_element_type=F32) * SCALE
        if last:
            copies[j].wait()
            for i, part in enumerate((dk, dv)):
                total = part + held[j, i]
                kept[j, i] = total[:half]
                send_ref[j, i] = total[half:].astype(BF)
            out_copies[j].start()
        else:
            held[j, 0] = dk
            held[j, 1] = dv
            copies[j].start()
        if j == 0:
            acc[...] = dq
        else:
            acc[...] += dq

    for b in range(blocks):
        place = lax.rem(at_ref[0] + blocks - b, blocks) if last else b
        for h in range(HQ):
            at = pl.ds((h * blocks + b) * rows, rows)
            dq_ref[place, :, h * DH : (h + 1) * DH] = acc[at, :].astype(BF)
    for copy in out_copies if last else copies:
        copy.wait()


def grads(place, x, kv, before=None):
    blocks, chunks = len(x), len(kv)
    rows, width = x[0].shape
    _, _, half, cols = kv[0].shape
    total = blocks * rows * HQ
    last = before is not None
    work = total * chunks * cols
    whole = pl.BlockSpec(memory_space=pltpu.VMEM)
    far = pl.BlockSpec(memory_space=pltpu.HBM)
    sums = (chunks, 2, 2 * half, cols)
    roomy = (SPARE * chunks,) + sums[1:]
    halves = (chunks, 2, half, cols)
    dq = jax.ShapeDtypeStruct((blocks, rows, WIDTH), BF)
    if last:
        operands = (place, *x, *kv, before)
        in_specs = [whole] * (len(operands) - 2) + [far]
        out_shape = [dq, jax.ShapeDtypeStruct(halves, F32), jax.ShapeDtypeStruct(halves, BF)]
        out_specs = [whole, far, whole]
        more = [pltpu.VMEM(halves, F32), pltpu.SemaphoreType.DMA((chunks,)), pltpu.SemaphoreType.DMA((chunks,))]
    else:
        operands = (place, x, *kv)
        in_specs = [whole] * (len(operands) - 1)
        out_shape = [dq, jax.ShapeDtypeStruct(roomy, F32)]
        out_specs = [whole, far]
        more = [pltpu.SemaphoreType.DMA((chunks,))]
    return pl.pallas_call(
        lambda *refs: grads_kernel(blocks, chunks, last, *refs),
        in_specs=[pl.BlockSpec(memory_space=pltpu.SMEM)] + in_specs,
        out_specs=out_specs,
        out_shape=out_shape,
        scratch_shapes=[
            pltpu.VMEM((total, 2 * DH), BF),
            pltpu.VMEM((total, 2 * DH), BF),
            pltpu.VMEM((total, DH), F32),
            pltpu.VMEM(sums, F32),
        ]
        + more,
        compiler_params=pltpu.CompilerParams(vmem_limit_bytes=VMEM_GRADS),
        cost_estimate=pl.CostEstimate(flops=10 * work * DH, bytes_accessed=4 << 20, transcendentals=work),
        name="grads",
    )(*operands)


def sum_kernel(parts_ref, out_ref):
    total = parts_ref[0].astype(F32)
    for b in range(1, parts_ref.shape[0]):
        total = total + parts_ref[b].astype(F32)
    out_ref[...] = total.astype(out_ref.dtype)


def total_of(parts, dtype):
    return pl.pallas_call(
        sum_kernel,
        out_shape=jax.ShapeDtypeStruct(parts.shape[1:], dtype),
        compiler_params=SMALL,
        name="total_of",
    )(parts)


def query_kernel(core_ref, parts_ref, far_ref, out_ref):
    core = core_ref[0]
    for h in range(HQ):
        at = pl.ds(h * DH, DH)
        total = far_ref[:, at].astype(F32)
        for b in range(parts_ref.shape[0]):
            total = total + parts_ref[b, :, at].astype(F32)
        out_ref[:, at] = half_swap(total, core).astype(BF)


def query_total(core, parts, far):
    return pl.pallas_call(
        query_kernel,
        in_specs=[pl.BlockSpec(memory_space=pltpu.SMEM)] + [pl.BlockSpec(memory_space=pltpu.VMEM)] * 2,
        out_shape=jax.ShapeDtypeStruct(far.shape, BF),
        compiler_params=SMALL,
        name="query_total",
    )(core, parts, far)


def both_kernel(keep_ref, got_ref, *refs):
    out_refs, (keep, got, sems) = refs[:-3], refs[-3:]
    copies = []
    for r in range(len(out_refs)):
        pair = (
            pltpu.make_async_copy(keep_ref.at[r], keep.at[r], sems.at[0, r]),
            pltpu.make_async_copy(got_ref.at[r], got.at[r], sems.at[1, r]),
        )
        for copy in pair:
            copy.start()
        copies.append(pair)
    for r, out_ref in enumerate(out_refs):
        for copy in copies[r]:
            copy.wait()
        out_ref[...] = (keep[r] + got[r].astype(F32)).astype(out_ref.dtype)


def both_cores(keep, got):
    count = keep.shape[0]
    one = jax.ShapeDtypeStruct(keep.shape[1:], BF)
    return pl.pallas_call(
        both_kernel,
        in_specs=[pl.BlockSpec(memory_space=pltpu.HBM)] * 2,
        out_shape=[one] * count,
        scratch_shapes=[
            pltpu.VMEM(keep.shape, keep.dtype),
            pltpu.VMEM(got.shape, got.dtype),
            pltpu.SemaphoreType.DMA((2, count)),
        ],
        compiler_params=MEDIUM,
        name="both_cores",
    )(keep, got)


def visual_kernel(*refs):
    parts = refs[:-2]
    for i, out_ref in enumerate(refs[-2:]):
        total = parts[0][i].astype(F32)
        for part in parts[1:]:
            total = total + part[i].astype(F32)
        out_ref[...] = total.astype(BF)


def visual_total(parts):
    one = jax.ShapeDtypeStruct(parts[0].shape[1:], BF)
    return pl.pallas_call(
        visual_kernel, out_shape=[one, one], compiler_params=SMALL, name="visual_total"
    )(*parts)


def along(axis, value, steps):
    count = lax.axis_size(axis)
    return lax.ppermute(value, axis, [(i, (i + steps) % count) for i in range(count)])


def to_quad(block):
    count = lax.axis_size("zi")
    return lax.all_to_all(jnp.broadcast_to(block, (count,) + block.shape), "zi", 0, 0)


def per_device(queries, keys, values, outputs, out_grad, logsumexp):
    core = lax.axis_index("core").astype(jnp.int32).reshape(1)
    x, kv = prep(core, queries, out_grad, outputs, logsumexp.T, keys, values)

    far = lax.ppermute(x, "zq", SWAP)
    kv = jnp.stack([kv, lax.ppermute(kv, "core", SWAP)])
    x_near = [x] + [along("zi", x, r) for r in range(1, lax.axis_size("zi"))]
    far, kv, x_near = lax.optimization_barrier((far, kv, x_near))
    kv = [kv] + [along("y", kv, -r) for r in range(1, lax.axis_size("y"))]
    x_far = to_quad(far)

    place = lax.axis_index("zi").astype(jnp.int32).reshape(1)
    dq_far, sums = grads(place, x_far, kv)
    far_parts = lax.all_to_all(dq_far, "zi", 0, 0)
    dq_near, keep, send = grads(place, x_near, kv, sums)
    far_parts, send, dq_near = lax.optimization_barrier((far_parts, send, dq_near))
    both = both_cores(keep, lax.ppermute(send, "core", SWAP))
    near_parts = lax.all_to_all(dq_near, "zi", 0, 0)
    far_sum = lax.ppermute(total_of(far_parts, BF), "zq", SWAP)
    query_grad = query_total(core, near_parts, far_sum)

    parts = [both[0]] + [along("y", both[r], r) for r in range(1, len(both))]
    key_grad, value_grad = visual_total(parts)
    return query_grad, key_grad, value_grad


def solution(mesh):
    devices = mesh.devices.reshape(2, 4, 2, 4, 2, 4)
    inner = Mesh(devices, ("zh", "x", "core", "y", "zq", "zi"))
    head = ("zh", "x", "core")
    seq = ("y", "zq", "zi")
    text = P(seq, head)
    visual = P(head, seq)
    return jax.shard_map(
        per_device,
        mesh=inner,
        in_specs=(text, visual, visual, text, text, text),
        out_specs=(text, visual, visual),
        check_vma=False,
    )
```

```python
import jax
import jax.numpy as jnp
from jax import lax
from jax.experimental import pallas as pl
from jax.experimental.pallas import tpu as pltpu
from jax.sharding import Mesh, PartitionSpec as P

DH = 128
HQ = 4
WIDTH = HQ * DH
SCALE = DH**-0.5
LOG2E = 1.4426950408889634
BF = jnp.bfloat16
F32 = jnp.float32
SWAP = [(0, 1), (1, 0)]
VMEM_GRADS = 40 << 20
SPARE = 10
MEDIUM = pltpu.CompilerParams(vmem_limit_bytes=12 << 20)
SMALL = pltpu.CompilerParams(vmem_limit_bytes=4 << 20)


def half_swap(value, core):
    rolled = jnp.concatenate([value[:, DH // 2 :], value[:, : DH // 2]], 1)
    return jnp.where(core == 0, value, rolled)


def prep_kernel(core_ref, q_ref, g_ref, o_ref, lse_ref, k_ref, v_ref, x_ref, copies_ref, kv_ref):
    core = core_ref[0]
    rows = q_ref.shape[0]
    lane = lax.broadcasted_iota(jnp.int32, (rows, DH), 1)
    lse = jnp.transpose(lse_ref[...]) * (-1.0 / SCALE)
    stats = jnp.zeros((rows, DH), F32)
    for h in range(HQ):
        at = pl.ds(h * DH, DH)
        q = q_ref[:, at].astype(F32)
        g = g_ref[:, at].astype(F32)
        dterm = jnp.sum(g * o_ref[:, at].astype(F32), axis=1, keepdims=True)
        mine = (lane & (HQ - 1)) == h
        stats = jnp.where(mine & (lane < 3 * HQ), lse[:, h : h + 1], stats)
        stats = jnp.where(mine & (lane >= 3 * HQ) & (lane < 6 * HQ), -dterm, stats)
        x_ref[:, at] = half_swap(q, core).astype(BF)
        x_ref[:, pl.ds(WIDTH + h * DH, DH)] = half_swap(g, core).astype(BF)
    high = stats.astype(BF).astype(F32)
    rest = stats - high
    middle = rest.astype(BF).astype(F32)
    group = lax.shift_right_logical(lane, 2)
    first = (group == 0) | (group == 3)
    second = (group == 1) | (group == 4)
    stats = jnp.where(first, high, jnp.where(second, middle, rest - middle))
    x_ref[:, pl.ds(2 * WIDTH, DH)] = stats.astype(BF)
    for b in range(copies_ref.shape[0]):
        copies_ref[b] = x_ref[...]
    kv_ref[0] = k_ref[...]
    kv_ref[1] = v_ref[...]


def prep(core, queries, out_grad, outputs, lse_t, keys, values):
    rows = queries.shape[0]
    return pl.pallas_call(
        prep_kernel,
        in_specs=[pl.BlockSpec(memory_space=pltpu.SMEM)] + [pl.BlockSpec(memory_space=pltpu.VMEM)] * 6,
        out_shape=[
            jax.ShapeDtypeStruct((rows, 2 * WIDTH + DH), BF),
            jax.ShapeDtypeStruct((lax.axis_size("zi"), rows, 2 * WIDTH + DH), BF),
            jax.ShapeDtypeStruct((2,) + keys.shape, BF),
        ],
        name="prep",
    )(core, queries, out_grad, outputs, lse_t, keys, values)


def grads_kernel(last, *refs):
    if last:
        quad_ref, x_ref, own_ref, other_ref, near_ref, before_ref, *refs = refs
        dq_ref, keep_ref, send_ref, q_s, g_s, acc, held, sems = refs
    else:
        x_ref, own_ref, other_ref, dq_ref, after_ref, q_s, g_s, acc, held, sems = refs
    blocks, rows, _ = x_ref.shape
    chunks, _, half, cols = own_ref.shape
    copies = []
    for j in range(chunks):
        ends = (before_ref.at[j], held.at[j]) if last else (held.at[j], after_ref.at[j])
        copies.append(pltpu.make_async_copy(*ends, sems.at[j]))
        if last:
            copies[j].start()
    lane = lax.broadcasted_iota(jnp.int32, (rows, DH), 1)
    for b in range(blocks):
        stats = x_ref[b, :, 2 * WIDTH : 2 * WIDTH + DH].astype(F32)
        for h in range(HQ):
            to = pl.ds((h * blocks + b) * rows, rows)
            mine = jnp.where((lane & (HQ - 1)) == h, stats, 0.0).astype(BF)
            q_s[to, :DH] = x_ref[b, :, h * DH : (h + 1) * DH]
            g_s[to, :DH] = x_ref[b, :, WIDTH + h * DH : WIDTH + (h + 1) * DH]
            q_s[to, DH:] = mine
            g_s[to, DH:] = mine

    row = lax.broadcasted_iota(jnp.int32, (DH, cols), 0)
    k_ones = jnp.where(row < 3 * HQ, 1.0, 0.0).astype(BF)
    v_ones = jnp.where((row >= 3 * HQ) & (row < 6 * HQ), 1.0, 0.0).astype(BF)
    over_rows = (((0,), (0,)), ((), ()))
    for j in range(chunks):
        k = jnp.concatenate([own_ref[j, 0], other_ref[j, 0]], 0)
        v = jnp.concatenate([own_ref[j, 1], other_ref[j, 1]], 0)
        s = jnp.dot(q_s[...], jnp.concatenate([k, k_ones], 0), preferred_element_type=F32)
        p = jnp.exp2(s * (SCALE * LOG2E))
        dp = jnp.dot(g_s[...], jnp.concatenate([v, v_ones], 0), preferred_element_type=F32)
        ds = (p * dp).astype(BF)
        pb = p.astype(BF)
        dv = lax.dot_general(g_s[:, :DH], pb, over_rows, preferred_element_type=F32)
        dk = lax.dot_general(q_s[:, :DH], ds, over_rows, preferred_element_type=F32) * SCALE
        dq = lax.dot_general(ds, k, (((1,), (1,)), ((), ())), preferred_element_type=F32) * SCALE
        if last:
            copies[j].wait()
            for i, part in enumerate((dk, dv)):
                total = part + held[j, i]
                keep_ref[j, i] = total[:half]
                send_ref[j, i] = total[half:].astype(BF)
        else:
            held[j, 0] = dk
            held[j, 1] = dv
            copies[j].start()
        if j == 0:
            acc[...] = dq
        else:
            acc[...] += dq

    out_ref = dq_ref
    if last:
        near = quad_ref[0]
        dq_ref[near] = near_ref[...]
        out_ref = dq_ref.at[1 - near]
    for b in range(blocks):
        for h in range(HQ):
            at = pl.ds((h * blocks + b) * rows, rows)
            out_ref[b, :, h * DH : (h + 1) * DH] = acc[at, :].astype(BF)
    if not last:
        for copy in copies:
            copy.wait()


def grads(x, own, other, quad=None, before=()):
    blocks, rows, _ = x.shape
    chunks, _, half, cols = own.shape
    total = blocks * rows * HQ
    last = quad is not None
    work = total * chunks * cols
    small = pl.BlockSpec(memory_space=pltpu.SMEM)
    whole = pl.BlockSpec(memory_space=pltpu.VMEM)
    far = pl.BlockSpec(memory_space=pltpu.HBM)
    sums = (chunks, 2, 2 * half, cols)
    halves = (chunks, 2, half, cols)
    if last:
        operands = (quad, x, own, other, *before)
        in_specs = [small] + [whole] * 4 + [far]
        out_shape = [
            jax.ShapeDtypeStruct((2, blocks, rows, WIDTH), BF),
            jax.ShapeDtypeStruct(halves, F32),
            jax.ShapeDtypeStruct(halves, BF),
        ]
        out_specs = [whole] * 3
    else:
        operands = (x, own, other)
        in_specs = [whole] * 3
        out_shape = [
            jax.ShapeDtypeStruct((blocks, rows, WIDTH), BF),
            jax.ShapeDtypeStruct((SPARE * chunks,) + sums[1:], F32),
        ]
        out_specs = [whole, far]
    return pl.pallas_call(
        lambda *refs: grads_kernel(last, *refs),
        in_specs=in_specs,
        out_specs=out_specs,
        out_shape=out_shape,
        scratch_shapes=[
            pltpu.VMEM((total, 2 * DH), BF),
            pltpu.VMEM((total, 2 * DH), BF),
            pltpu.VMEM((total, DH), F32),
            pltpu.VMEM(sums, F32),
            pltpu.SemaphoreType.DMA((chunks,)),
        ],
        compiler_params=pltpu.CompilerParams(vmem_limit_bytes=VMEM_GRADS),
        cost_estimate=pl.CostEstimate(flops=10 * work * DH, bytes_accessed=4 << 20, transcendentals=work),
        name="grads",
    )(*operands)


def query_kernel(core_ref, parts_ref, out_ref):
    core = core_ref[0]
    for h in range(HQ):
        at = pl.ds(h * DH, DH)
        total = parts_ref[0, :, at].astype(F32)
        for b in range(1, parts_ref.shape[0]):
            total = total + parts_ref[b, :, at].astype(F32)
        out_ref[:, at] = half_swap(total, core).astype(BF)


def query_total(core, parts):
    return pl.pallas_call(
        query_kernel,
        in_specs=[pl.BlockSpec(memory_space=pltpu.SMEM), pl.BlockSpec(memory_space=pltpu.VMEM)],
        out_shape=jax.ShapeDtypeStruct(parts.shape[1:], BF),
        compiler_params=SMALL,
        name="query_total",
    )(core, parts)


def both_kernel(y_ref, keep_ref, got_ref, *out_refs):
    count = len(out_refs)
    for r, out_ref in enumerate(out_refs):
        at = lax.rem(y_ref[0] + r, count)
        out_ref[...] = (keep_ref[at] + got_ref[at].astype(F32)).astype(out_ref.dtype)


def both_cores(y, keep, got):
    one = jax.ShapeDtypeStruct(keep.shape[1:], BF)
    return pl.pallas_call(
        both_kernel,
        in_specs=[pl.BlockSpec(memory_space=pltpu.SMEM)] + [pl.BlockSpec(memory_space=pltpu.VMEM)] * 2,
        out_shape=[one] * keep.shape[0],
        compiler_params=MEDIUM,
        name="both_cores",
    )(y, keep, got)


def visual_kernel(*refs):
    parts = refs[:-2]
    for i, out_ref in enumerate(refs[-2:]):
        total = parts[0][i].astype(F32)
        for part in parts[1:]:
            total = total + part[i].astype(F32)
        out_ref[...] = total.astype(BF)


def visual_total(parts):
    one = jax.ShapeDtypeStruct(parts[0].shape[1:], BF)
    return pl.pallas_call(
        visual_kernel, out_shape=[one, one], compiler_params=SMALL, name="visual_total"
    )(*parts)


def along(axis, value, steps):
    count = lax.axis_size(axis)
    return lax.ppermute(value, axis, [(i, (i + steps) % count) for i in range(count)])


def index(axis):
    return lax.axis_index(axis).astype(jnp.int32).reshape(1)


def per_device(queries, keys, values, outputs, out_grad, logsumexp):
    core = index("core")
    x, copies, kv = prep(core, queries, out_grad, outputs, logsumexp.T, keys, values)

    x_near = lax.all_to_all(copies, "zi", 0, 0)
    far = lax.ppermute(x, "zq", SWAP)

    own = lax.all_gather(kv, "y")
    far, own = lax.optimization_barrier((far, own))
    other = lax.ppermute(own, "core", SWAP)
    x_far = lax.all_to_all(jnp.broadcast_to(far, copies.shape), "zi", 0, 0)

    before = grads(x_near, own, other)
    dq, keep, send = grads(x_far, own, other, index("zq"), before)
    dq = dq.reshape((-1,) + dq.shape[2:])
    query_grad = query_total(core, lax.all_to_all(dq, ("zq", "zi"), 0, 0))

    both = both_cores(index("y"), keep, lax.ppermute(send, "core", SWAP))
    parts = [both[0]] + [along("y", both[r], r) for r in range(1, len(both))]
    key_grad, value_grad = visual_total(parts)
    return query_grad, key_grad, value_grad


def solution(mesh):
    devices = mesh.devices.reshape(2, 4, 2, 4, 2, 4)
    inner = Mesh(devices, ("zh", "x", "core", "y", "zq", "zi"))
    head = ("zh", "x", "core")
    seq = ("y", "zq", "zi")
    text = P(seq, head)
    visual = P(head, seq)
    return jax.shard_map(
        per_device,
        mesh=inner,
        in_specs=(text, visual, visual, text, text, text),
        out_specs=(text, visual, visual),
        check_vma=False,
    )
```

```python
import jax
import jax.numpy as jnp
from jax import lax
from jax.experimental import pallas as pl
from jax.experimental.pallas import tpu as pltpu
from jax.sharding import Mesh, PartitionSpec as P

DH = 128
HQ = 4
WIDTH = HQ * DH
STATS = 4 * HQ
SCALE = DH**-0.5
LOG2E = 1.4426950408889634
BF = jnp.bfloat16
F32 = jnp.float32
SWAP = [(0, 1), (1, 0)]
VMEM_GRADS = 40 << 20
SPARE = 10
MEDIUM = pltpu.CompilerParams(vmem_limit_bytes=12 << 20)
SMALL = pltpu.CompilerParams(vmem_limit_bytes=4 << 20)


def half_swap(value, core):
    rolled = jnp.concatenate([value[:, DH // 2 :], value[:, : DH // 2]], 1)
    return jnp.where(core == 0, value, rolled)


def prep_kernel(core_ref, q_ref, g_ref, o_ref, lse_ref, k_ref, v_ref, copies_ref, kv_ref):
    core = core_ref[0]
    rows = q_ref.shape[0]
    lane = lax.broadcasted_iota(jnp.int32, (rows, DH), 1)
    lse = jnp.transpose(lse_ref[...]) * (-1.0 / SCALE)
    stats = jnp.zeros((rows, DH), F32)
    block = copies_ref.at[0]
    for h in range(HQ):
        at = pl.ds(h * DH, DH)
        q = q_ref[:, at].astype(F32)
        g = g_ref[:, at].astype(F32)
        dterm = jnp.sum(g * o_ref[:, at].astype(F32), axis=1, keepdims=True)
        mine = (lane & (HQ - 1)) == h
        stats = jnp.where(mine & (lane < 2 * HQ), lse[:, h : h + 1], stats)
        stats = jnp.where(mine & (lane >= 2 * HQ) & (lane < STATS), -dterm, stats)
        block[h * rows : (h + 1) * rows, :] = half_swap(q, core).astype(BF)
        block[(HQ + h) * rows : (HQ + h + 1) * rows, :] = half_swap(g, core).astype(BF)
    high = stats.astype(BF).astype(F32)
    stats = jnp.where((lane & HQ) == 0, high, stats - high)
    stats = jnp.concatenate([stats, jnp.zeros((DH - rows, DH), F32)], 0)
    block[2 * HQ * rows :, :] = jnp.transpose(stats)[:STATS].astype(BF)
    for b in range(1, copies_ref.shape[0]):
        copies_ref[b] = copies_ref[0]
    kv_ref[0] = k_ref[...]
    kv_ref[1] = v_ref[...]


def prep(core, queries, out_grad, outputs, lse_t, keys, values):
    rows = queries.shape[0]
    return pl.pallas_call(
        prep_kernel,
        in_specs=[pl.BlockSpec(memory_space=pltpu.SMEM)] + [pl.BlockSpec(memory_space=pltpu.VMEM)] * 6,
        out_shape=[
            jax.ShapeDtypeStruct((lax.axis_size("z4"), 2 * HQ * rows + STATS, DH), BF),
            jax.ShapeDtypeStruct((2,) + keys.shape, BF),
        ],
        name="prep",
    )(core, queries, out_grad, outputs, lse_t, keys, values)


def grads_kernel(last, *refs):
    if last:
        side_ref, x_ref, own_ref, other_ref, near_ref, before_ref, *refs = refs
        dq_ref, keep_ref, send_ref, q_s, g_s, acc, held, sems = refs
    else:
        x_ref, own_ref, other_ref, dq_ref, after_ref, q_s, g_s, acc, held, sems = refs
    blocks = x_ref.shape[0]
    rows = (x_ref.shape[1] - STATS) // (2 * HQ)
    chunks, _, half, cols = own_ref.shape
    copies = []
    for j in range(chunks):
        ends = (before_ref.at[j], held.at[j]) if last else (held.at[j], after_ref.at[j])
        copies.append(pltpu.make_async_copy(*ends, sems.at[j]))
        if last:
            copies[j].start()
    lane = lax.broadcasted_iota(jnp.int32, (rows, DH), 1)
    for b in range(blocks):
        stats = x_ref[b, 2 * HQ * rows :, :].astype(F32)
        stats = jnp.concatenate([stats, jnp.zeros((DH - STATS, DH), F32)], 0)
        stats = jnp.transpose(stats)[:rows]
        for h in range(HQ):
            to = pl.ds((h * blocks + b) * rows, rows)
            mine = jnp.where((lane & (HQ - 1)) == h, stats, 0.0).astype(BF)
            q_s[to, :DH] = x_ref[b, h * rows : (h + 1) * rows, :]
            g_s[to, :DH] = x_ref[b, (HQ + h) * rows : (HQ + h + 1) * rows, :]
            q_s[to, DH:] = mine
            g_s[to, DH:] = mine

    row = lax.broadcasted_iota(jnp.int32, (DH, cols), 0)
    k_ones = jnp.where(row < STATS // 2, 1.0, 0.0).astype(BF)
    v_ones = jnp.where((row >= STATS // 2) & (row < STATS), 1.0, 0.0).astype(BF)
    over_rows = (((0,), (0,)), ((), ()))
    for j in range(chunks):
        k = jnp.concatenate([own_ref[j, 0], other_ref[j, 0]], 0)
        v = jnp.concatenate([own_ref[j, 1], other_ref[j, 1]], 0)
        s = jnp.dot(q_s[...], jnp.concatenate([k, k_ones], 0), preferred_element_type=F32)
        p = jnp.exp2(s * (SCALE * LOG2E))
        dp = jnp.dot(g_s[...], jnp.concatenate([v, v_ones], 0), preferred_element_type=F32)
        ds = (p * dp).astype(BF)
        pb = p.astype(BF)
        dv = lax.dot_general(g_s[:, :DH], pb, over_rows, preferred_element_type=F32)
        dk = lax.dot_general(q_s[:, :DH], ds, over_rows, preferred_element_type=F32) * SCALE
        dq = lax.dot_general(ds, k, (((1,), (1,)), ((), ())), preferred_element_type=F32) * SCALE
        if last:
            copies[j].wait()
            for i, part in enumerate((dk, dv)):
                total = part + held[j, i]
                keep_ref[j, i] = total[:half]
                send_ref[j, i] = total[half:].astype(BF)
        else:
            held[j, 0] = dk
            held[j, 1] = dv
            copies[j].start()
        if j == 0:
            acc[...] = dq
        else:
            acc[...] += dq

    if last:
        side = side_ref[0]
        for b in range(blocks):
            dq_ref[b, side] = near_ref[b]
    for b in range(blocks):
        out_ref = dq_ref.at[b, 1 - side] if last else dq_ref.at[b]
        for h in range(HQ):
            at = pl.ds((h * blocks + b) * rows, rows)
            out_ref[:, h * DH : (h + 1) * DH] = acc[at, :].astype(BF)
    if not last:
        for copy in copies:
            copy.wait()


def grads(x, own, other, side=None, before=()):
    blocks = x.shape[0]
    rows = (x.shape[1] - STATS) // (2 * HQ)
    chunks, _, half, cols = own.shape
    total = blocks * rows * HQ
    last = side is not None
    work = total * chunks * cols
    small = pl.BlockSpec(memory_space=pltpu.SMEM)
    whole = pl.BlockSpec(memory_space=pltpu.VMEM)
    far = pl.BlockSpec(memory_space=pltpu.HBM)
    sums = (chunks, 2, 2 * half, cols)
    halves = (chunks, 2, half, cols)
    if last:
        operands = (side, x, own, other, *before)
        in_specs = [small] + [whole] * 4 + [far]
        out_shape = [
            jax.ShapeDtypeStruct((blocks, 2, rows, WIDTH), BF),
            jax.ShapeDtypeStruct(halves, F32),
            jax.ShapeDtypeStruct(halves, BF),
        ]
        out_specs = [whole] * 3
    else:
        operands = (x, own, other)
        in_specs = [whole] * 3
        out_shape = [
            jax.ShapeDtypeStruct((blocks, rows, WIDTH), BF),
            jax.ShapeDtypeStruct((SPARE * chunks,) + sums[1:], F32),
        ]
        out_specs = [whole, far]
    return pl.pallas_call(
        lambda *refs: grads_kernel(last, *refs),
        in_specs=in_specs,
        out_specs=out_specs,
        out_shape=out_shape,
        scratch_shapes=[
            pltpu.VMEM((total, 2 * DH), BF),
            pltpu.VMEM((total, 2 * DH), BF),
            pltpu.VMEM((total, DH), F32),
            pltpu.VMEM(sums, F32),
            pltpu.SemaphoreType.DMA((chunks,)),
        ],
        compiler_params=pltpu.CompilerParams(vmem_limit_bytes=VMEM_GRADS),
        cost_estimate=pl.CostEstimate(flops=10 * work * DH, bytes_accessed=4 << 20, transcendentals=work),
        name="grads",
    )(*operands)


def query_kernel(core_ref, parts_ref, out_ref):
    core = core_ref[0]
    for h in range(HQ):
        at = pl.ds(h * DH, DH)
        total = parts_ref[0, :, at].astype(F32)
        for b in range(1, parts_ref.shape[0]):
            total = total + parts_ref[b, :, at].astype(F32)
        out_ref[:, at] = half_swap(total, core).astype(BF)


def query_total(core, parts):
    return pl.pallas_call(
        query_kernel,
        in_specs=[pl.BlockSpec(memory_space=pltpu.SMEM), pl.BlockSpec(memory_space=pltpu.VMEM)],
        out_shape=jax.ShapeDtypeStruct(parts.shape[1:], BF),
        compiler_params=SMALL,
        name="query_total",
    )(core, parts)


def both_kernel(y_ref, keep_ref, got_ref, *out_refs):
    count = len(out_refs)
    for r, out_ref in enumerate(out_refs):
        at = lax.rem(y_ref[0] + r, count)
        out_ref[...] = (keep_ref[at] + got_ref[at].astype(F32)).astype(out_ref.dtype)


def both_cores(y, keep, got):
    one = jax.ShapeDtypeStruct(keep.shape[1:], BF)
    return pl.pallas_call(
        both_kernel,
        in_specs=[pl.BlockSpec(memory_space=pltpu.SMEM)] + [pl.BlockSpec(memory_space=pltpu.VMEM)] * 2,
        out_shape=[one] * keep.shape[0],
        compiler_params=MEDIUM,
        name="both_cores",
    )(y, keep, got)


def visual_kernel(*refs):
    parts = refs[:-2]
    for i, out_ref in enumerate(refs[-2:]):
        total = parts[0][i].astype(F32)
        for part in parts[1:]:
            total = total + part[i].astype(F32)
        out_ref[...] = total.astype(BF)


def visual_total(parts):
    one = jax.ShapeDtypeStruct(parts[0].shape[1:], BF)
    return pl.pallas_call(
        visual_kernel, out_shape=[one, one], compiler_params=SMALL, name="visual_total"
    )(*parts)


def along(axis, value, steps):
    count = lax.axis_size(axis)
    return lax.ppermute(value, axis, [(i, (i + steps) % count) for i in range(count)])


def index(axis):
    return lax.axis_index(axis).astype(jnp.int32).reshape(1)


def per_device(queries, keys, values, outputs, out_grad, logsumexp):
    core = index("core")
    copies, kv = prep(core, queries, out_grad, outputs, logsumexp.T, keys, values)

    x = lax.all_to_all(copies, "z4", 0, 0)

    own = lax.all_gather(kv, "y")
    other = lax.ppermute(own, "core", SWAP)
    x, own, other = lax.optimization_barrier((x, own, other))
    beside = lax.ppermute(x, "z2", SWAP)

    before = grads(x, own, other)
    dq, keep, send = grads(beside, own, other, index("z2"), before)
    dq = dq.reshape((-1,) + dq.shape[2:])
    query_grad = query_total(core, lax.all_to_all(dq, ("z4", "z2"), 0, 0))

    both = both_cores(index("y"), keep, lax.ppermute(send, "core", SWAP))
    parts = [both[0]] + [along("y", both[r], r) for r in range(1, len(both))]
    key_grad, value_grad = visual_total(parts)
    return query_grad, key_grad, value_grad


def solution(mesh):
    devices = mesh.devices.reshape(2, 4, 2, 4, 4, 2)
    inner = Mesh(devices, ("zh", "x", "core", "y", "z4", "z2"))
    head = ("zh", "x", "core")
    seq = ("y", "z4", "z2")
    text = P(seq, head)
    visual = P(head, seq)
    return jax.shard_map(
        per_device,
        mesh=inner,
        in_specs=(text, visual, visual, text, text, text),
        out_specs=(text, visual, visual),
        check_vma=False,
    )
```

```python
import jax
import jax.numpy as jnp
from jax import lax
from jax.experimental import pallas as pl
from jax.experimental.pallas import tpu as pltpu
from jax.sharding import Mesh, PartitionSpec as P

DH = 128
HQ = 4
WIDTH = HQ * DH
STATS = 4 * HQ
SCALE = DH**-0.5
LOG2E = 1.4426950408889634
BF = jnp.bfloat16
F32 = jnp.float32
SWAP = [(0, 1), (1, 0)]
VMEM_GRADS = 40 << 20
SPARE = 10
MEDIUM = pltpu.CompilerParams(vmem_limit_bytes=12 << 20)
SMALL = pltpu.CompilerParams(vmem_limit_bytes=4 << 20)


def half_swap(value, core):
    rolled = jnp.concatenate([value[:, DH // 2 :], value[:, : DH // 2]], 1)
    return jnp.where(core == 0, value, rolled)


def prep_kernel(core_ref, q_ref, g_ref, o_ref, lse_ref, k_ref, v_ref, x_ref, copies_ref, kv_ref):
    core = core_ref[0]
    rows = q_ref.shape[0]
    lane = lax.broadcasted_iota(jnp.int32, (rows, DH), 1)
    lse = jnp.transpose(lse_ref[...]) * (-1.0 / SCALE)
    stats = jnp.zeros((rows, DH), F32)
    for h in range(HQ):
        at = pl.ds(h * DH, DH)
        q = q_ref[:, at].astype(F32)
        g = g_ref[:, at].astype(F32)
        dterm = jnp.sum(g * o_ref[:, at].astype(F32), axis=1, keepdims=True)
        mine = (lane & (HQ - 1)) == h
        stats = jnp.where(mine & (lane < 2 * HQ), lse[:, h : h + 1], stats)
        stats = jnp.where(mine & (lane >= 2 * HQ) & (lane < STATS), -dterm, stats)
        x_ref[h * rows : (h + 1) * rows, :] = half_swap(q, core).astype(BF)
        x_ref[(HQ + h) * rows : (HQ + h + 1) * rows, :] = half_swap(g, core).astype(BF)
    high = stats.astype(BF).astype(F32)
    stats = jnp.where((lane & HQ) == 0, high, stats - high)
    stats = jnp.concatenate([stats, jnp.zeros((DH - rows, DH), F32)], 0)
    x_ref[2 * HQ * rows :, :] = jnp.transpose(stats)[:STATS].astype(BF)
    for b in range(copies_ref.shape[0]):
        copies_ref[b] = x_ref[...]
    kv_ref[0] = k_ref[...]
    kv_ref[1] = v_ref[...]


def prep(core, queries, out_grad, outputs, lse_t, keys, values):
    rows = queries.shape[0]
    return pl.pallas_call(
        prep_kernel,
        in_specs=[pl.BlockSpec(memory_space=pltpu.SMEM)] + [pl.BlockSpec(memory_space=pltpu.VMEM)] * 6,
        out_shape=[
            jax.ShapeDtypeStruct((2 * HQ * rows + STATS, DH), BF),
            jax.ShapeDtypeStruct((lax.axis_size("zi"), 2 * HQ * rows + STATS, DH), BF),
            jax.ShapeDtypeStruct((2,) + keys.shape, BF),
        ],
        name="prep",
    )(core, queries, out_grad, outputs, lse_t, keys, values)


def grads_kernel(last, *refs):
    if last:
        side_ref, x_ref, own_ref, other_ref, near_ref, before_ref, *refs = refs
        dq_ref, keep_ref, send_ref, q_s, g_s, acc, held, sems, got = refs
    else:
        x_ref, own_ref, other_ref, dq_ref, after_ref, q_s, g_s, acc, held, sems = refs
    blocks = x_ref.shape[0]
    rows = (x_ref.shape[1] - STATS) // (2 * HQ)
    chunks, _, half, cols = own_ref.shape
    copies = []
    for j in range(chunks):
        ends = (before_ref.at[j], got.at[j]) if last else (held.at[j], after_ref.at[j])
        copies.append(pltpu.make_async_copy(*ends, sems.at[j]))
        if last:
            copies[j].start()
    lane = lax.broadcasted_iota(jnp.int32, (rows, DH), 1)
    for b in range(blocks):
        stats = x_ref[b, 2 * HQ * rows :, :].astype(F32)
        stats = jnp.concatenate([stats, jnp.zeros((DH - STATS, DH), F32)], 0)
        stats = jnp.transpose(stats)[:rows]
        for h in range(HQ):
            to = pl.ds((h * blocks + b) * rows, rows)
            mine = jnp.where((lane & (HQ - 1)) == h, stats, 0.0).astype(BF)
            q_s[to, :DH] = x_ref[b, h * rows : (h + 1) * rows, :]
            g_s[to, :DH] = x_ref[b, (HQ + h) * rows : (HQ + h + 1) * rows, :]
            q_s[to, DH:] = mine
            g_s[to, DH:] = mine

    row = lax.broadcasted_iota(jnp.int32, (DH, cols), 0)
    k_ones = jnp.where(row < STATS // 2, 1.0, 0.0).astype(BF)
    v_ones = jnp.where((row >= STATS // 2) & (row < STATS), 1.0, 0.0).astype(BF)
    over_rows = (((0,), (0,)), ((), ()))
    for j in range(chunks):
        k = jnp.concatenate([own_ref[j, 0], other_ref[j, 0]], 0)
        v = jnp.concatenate([own_ref[j, 1], other_ref[j, 1]], 0)
        s = jnp.dot(q_s[...], jnp.concatenate([k, k_ones], 0), preferred_element_type=F32)
        p = jnp.exp2(s * (SCALE * LOG2E))
        dp = jnp.dot(g_s[...], jnp.concatenate([v, v_ones], 0), preferred_element_type=F32)
        ds = (p * dp).astype(BF)
        pb = p.astype(BF)
        dv = lax.dot_general(g_s[:, :DH], pb, over_rows, preferred_element_type=F32)
        dk = lax.dot_general(q_s[:, :DH], ds, over_rows, preferred_element_type=F32) * SCALE
        dq = lax.dot_general(ds, k, (((1,), (1,)), ((), ())), preferred_element_type=F32) * SCALE
        held[j, 0] = dk
        held[j, 1] = dv
        if not last:
            copies[j].start()
        if j == 0:
            acc[...] = dq
        else:
            acc[...] += dq

    if last:
        side = side_ref[0]
        dq_ref[side] = near_ref[...]
    for b in range(blocks):
        out_ref = dq_ref.at[1 - side, b] if last else dq_ref.at[b]
        for h in range(HQ):
            at = pl.ds((h * blocks + b) * rows, rows)
            out_ref[:, h * DH : (h + 1) * DH] = acc[at, :].astype(BF)
    for j, copy in enumerate(copies):
        copy.wait()
        if last:
            total = held[j] + got[j]
            keep_ref[j] = total[:, :half]
            send_ref[j] = total[:, half:].astype(BF)


def grads(x, own, other, side=None, before=()):
    blocks = x.shape[0]
    rows = (x.shape[1] - STATS) // (2 * HQ)
    chunks, _, half, cols = own.shape
    total = blocks * rows * HQ
    last = side is not None
    work = total * chunks * cols
    small = pl.BlockSpec(memory_space=pltpu.SMEM)
    whole = pl.BlockSpec(memory_space=pltpu.VMEM)
    far = pl.BlockSpec(memory_space=pltpu.HBM)
    sums = (chunks, 2, 2 * half, cols)
    halves = (chunks, 2, half, cols)
    if last:
        operands = (side, x, own, other, *before)
        in_specs = [small] + [whole] * 4 + [far]
        out_shape = [
            jax.ShapeDtypeStruct((2, blocks, rows, WIDTH), BF),
            jax.ShapeDtypeStruct(halves, F32),
            jax.ShapeDtypeStruct(halves, BF),
        ]
        out_specs = [whole] * 3
    else:
        operands = (x, own, other)
        in_specs = [whole] * 3
        out_shape = [
            jax.ShapeDtypeStruct((blocks, rows, WIDTH), BF),
            jax.ShapeDtypeStruct((SPARE * chunks,) + sums[1:], F32),
        ]
        out_specs = [whole, far]
    return pl.pallas_call(
        lambda *refs: grads_kernel(last, *refs),
        in_specs=in_specs,
        out_specs=out_specs,
        out_shape=out_shape,
        scratch_shapes=[
            pltpu.VMEM((total, 2 * DH), BF),
            pltpu.VMEM((total, 2 * DH), BF),
            pltpu.VMEM((total, DH), F32),
            pltpu.VMEM(sums, F32),
            pltpu.SemaphoreType.DMA((chunks,)),
        ]
        + [pltpu.VMEM(sums, F32)] * last,
        compiler_params=pltpu.CompilerParams(vmem_limit_bytes=VMEM_GRADS),
        cost_estimate=pl.CostEstimate(flops=10 * work * DH, bytes_accessed=4 << 20, transcendentals=work),
        name="grads",
    )(*operands)


def query_kernel(core_ref, parts_ref, out_ref):
    core = core_ref[0]
    for h in range(HQ):
        at = pl.ds(h * DH, DH)
        total = parts_ref[0, :, at].astype(F32)
        for b in range(1, parts_ref.shape[0]):
            total = total + parts_ref[b, :, at].astype(F32)
        out_ref[:, at] = half_swap(total, core).astype(BF)


def query_total(core, parts):
    return pl.pallas_call(
        query_kernel,
        in_specs=[pl.BlockSpec(memory_space=pltpu.SMEM), pl.BlockSpec(memory_space=pltpu.VMEM)],
        out_shape=jax.ShapeDtypeStruct(parts.shape[1:], BF),
        compiler_params=SMALL,
        name="query_total",
    )(core, parts)


def both_kernel(y_ref, keep_ref, got_ref, *out_refs):
    count = len(out_refs)
    for r, out_ref in enumerate(out_refs):
        at = lax.rem(y_ref[0] + r, count)
        out_ref[...] = (keep_ref[at] + got_ref[at].astype(F32)).astype(out_ref.dtype)


def both_cores(y, keep, got):
    one = jax.ShapeDtypeStruct(keep.shape[1:], BF)
    return pl.pallas_call(
        both_kernel,
        in_specs=[pl.BlockSpec(memory_space=pltpu.SMEM)] + [pl.BlockSpec(memory_space=pltpu.VMEM)] * 2,
        out_shape=[one] * keep.shape[0],
        compiler_params=MEDIUM,
        name="both_cores",
    )(y, keep, got)


def visual_kernel(*refs):
    parts = refs[:-2]
    for i, out_ref in enumerate(refs[-2:]):
        total = parts[0][i].astype(F32)
        for part in parts[1:]:
            total = total + part[i].astype(F32)
        out_ref[...] = total.astype(BF)


def visual_total(parts):
    one = jax.ShapeDtypeStruct(parts[0].shape[1:], BF)
    return pl.pallas_call(
        visual_kernel, out_shape=[one, one], compiler_params=SMALL, name="visual_total"
    )(*parts)


def along(axis, value, steps):
    count = lax.axis_size(axis)
    return lax.ppermute(value, axis, [(i, (i + steps) % count) for i in range(count)])


def index(axis):
    return lax.axis_index(axis).astype(jnp.int32).reshape(1)


def per_device(queries, keys, values, outputs, out_grad, logsumexp):
    core = index("core")
    x, copies, kv = prep(core, queries, out_grad, outputs, logsumexp.T, keys, values)

    far = lax.ppermute(x, "zq", SWAP)
    x_near = lax.all_to_all(copies, "zi", 0, 0)

    own = lax.all_gather(kv, "y")
    far, own = lax.optimization_barrier((far, own))
    other = lax.ppermute(own, "core", SWAP)
    x_far = lax.all_to_all(jnp.broadcast_to(far, copies.shape), "zi", 0, 0)

    before = grads(x_near, own, other)
    dq, keep, send = grads(x_far, own, other, index("zq"), before)
    dq = dq.reshape((-1,) + dq.shape[2:])
    query_grad = query_total(core, lax.all_to_all(dq, ("zq", "zi"), 0, 0))

    both = both_cores(index("y"), keep, lax.ppermute(send, "core", SWAP))
    parts = [both[0]] + [along("y", both[r], r) for r in (1, 3, 2)]
    key_grad, value_grad = visual_total(parts)
    return query_grad, key_grad, value_grad


def solution(mesh):
    devices = mesh.devices.reshape(2, 4, 2, 4, 2, 4)
    inner = Mesh(devices, ("zh", "x", "core", "y", "zq", "zi"))
    head = ("zh", "x", "core")
    seq = ("y", "zq", "zi")
    text = P(seq, head)
    visual = P(head, seq)
    return jax.shard_map(
        per_device,
        mesh=inner,
        in_specs=(text, visual, visual, text, text, text),
        out_specs=(text, visual, visual),
        check_vma=False,
    )
```

```python
import jax
import jax.numpy as jnp
from jax import lax
from jax.experimental import pallas as pl
from jax.experimental.pallas import tpu as pltpu
from jax.sharding import Mesh, PartitionSpec as P

DH = 128
HQ = 4
WIDTH = HQ * DH
STATS = 4 * HQ
GROUP = 2
SCALE = DH**-0.5
LOG2E = 1.4426950408889634
BF = jnp.bfloat16
F32 = jnp.float32
SWAP = [(0, 1), (1, 0)]
VMEM_GRADS = 40 << 20
SPARE = 10
MEDIUM = pltpu.CompilerParams(vmem_limit_bytes=12 << 20)
SMALL = pltpu.CompilerParams(vmem_limit_bytes=4 << 20)


def half_swap(value, core):
    rolled = jnp.concatenate([value[:, DH // 2 :], value[:, : DH // 2]], 1)
    return jnp.where(core == 0, value, rolled)


def prep_kernel(core_ref, q_ref, g_ref, o_ref, lse_ref, k_ref, v_ref, x_ref, copies_ref, kv_ref):
    core = core_ref[0]
    rows = q_ref.shape[0]
    lane = lax.broadcasted_iota(jnp.int32, (rows, DH), 1)
    lse = jnp.transpose(lse_ref[...]) * (-1.0 / SCALE)
    stats = jnp.zeros((rows, DH), F32)
    for h in range(HQ):
        at = pl.ds(h * DH, DH)
        q = q_ref[:, at].astype(F32)
        g = g_ref[:, at].astype(F32)
        dterm = jnp.sum(g * o_ref[:, at].astype(F32), axis=1, keepdims=True)
        mine = (lane & (HQ - 1)) == h
        stats = jnp.where(mine & (lane < 2 * HQ), lse[:, h : h + 1], stats)
        stats = jnp.where(mine & (lane >= 2 * HQ) & (lane < STATS), -dterm, stats)
        x_ref[h * rows : (h + 1) * rows, :] = half_swap(q, core).astype(BF)
        x_ref[(HQ + h) * rows : (HQ + h + 1) * rows, :] = half_swap(g, core).astype(BF)
    high = stats.astype(BF).astype(F32)
    stats = jnp.where((lane & HQ) == 0, high, stats - high)
    stats = jnp.concatenate([stats, jnp.zeros((DH - rows, DH), F32)], 0)
    x_ref[2 * HQ * rows :, :] = jnp.transpose(stats)[:STATS].astype(BF)
    for b in range(copies_ref.shape[0]):
        copies_ref[b] = x_ref[...]
    kv_ref[0] = k_ref[...]
    kv_ref[1] = v_ref[...]


def prep(core, queries, out_grad, outputs, lse_t, keys, values):
    rows = queries.shape[0]
    return pl.pallas_call(
        prep_kernel,
        in_specs=[pl.BlockSpec(memory_space=pltpu.SMEM)] + [pl.BlockSpec(memory_space=pltpu.VMEM)] * 6,
        out_shape=[
            jax.ShapeDtypeStruct((2 * HQ * rows + STATS, DH), BF),
            jax.ShapeDtypeStruct((lax.axis_size("zi"), 2 * HQ * rows + STATS, DH), BF),
            jax.ShapeDtypeStruct((2,) + keys.shape, BF),
        ],
        name="prep",
    )(core, queries, out_grad, outputs, lse_t, keys, values)


def grads_kernel(last, *refs):
    if last:
        x_ref, own_ref, other_ref, near_ref, before_ref, *refs = refs
        dq_ref, keep_ref, send_ref, q_s, g_s, acc, held, sems, got = refs
    else:
        x_ref, own_ref, other_ref, dq_ref, after_ref, q_s, g_s, acc, held, sems = refs
    blocks = x_ref.shape[0]
    rows = (x_ref.shape[1] - STATS) // (2 * HQ)
    chunks, _, half, cols = own_ref.shape
    copies = []
    for j in range(chunks):
        ends = (before_ref.at[j], got.at[j]) if last else (held.at[j], after_ref.at[j])
        copies.append(pltpu.make_async_copy(*ends, sems.at[j]))
        if last:
            copies[j].start()
    lane = lax.broadcasted_iota(jnp.int32, (rows, DH), 1)
    for b in range(blocks):
        stats = x_ref[b, 2 * HQ * rows :, :].astype(F32)
        stats = jnp.concatenate([stats, jnp.zeros((DH - STATS, DH), F32)], 0)
        stats = jnp.transpose(stats)[:rows]
        for h in range(HQ):
            to = pl.ds((h * blocks + b) * rows, rows)
            mine = jnp.where((lane & (HQ - 1)) == h, stats, 0.0).astype(BF)
            q_s[to, :DH] = x_ref[b, h * rows : (h + 1) * rows, :]
            g_s[to, :DH] = x_ref[b, (HQ + h) * rows : (HQ + h + 1) * rows, :]
            q_s[to, DH:] = mine
            g_s[to, DH:] = mine

    row = lax.broadcasted_iota(jnp.int32, (DH, GROUP * cols), 0)
    k_ones = jnp.where(row < STATS // 2, 1.0, 0.0).astype(BF)
    v_ones = jnp.where((row >= STATS // 2) & (row < STATS), 1.0, 0.0).astype(BF)
    over_rows = (((0,), (0,)), ((), ()))
    for j in range(0, chunks, GROUP):
        group = range(j, j + GROUP)
        k = jnp.concatenate([jnp.concatenate([own_ref[i, 0], other_ref[i, 0]], 0) for i in group], 1)
        v = jnp.concatenate([jnp.concatenate([own_ref[i, 1], other_ref[i, 1]], 0) for i in group], 1)
        s = jnp.dot(q_s[...], jnp.concatenate([k, k_ones], 0), preferred_element_type=F32)
        p = jnp.exp2(s * (SCALE * LOG2E))
        dp = jnp.dot(g_s[...], jnp.concatenate([v, v_ones], 0), preferred_element_type=F32)
        ds = (p * dp).astype(BF)
        pb = p.astype(BF)
        dv = lax.dot_general(g_s[:, :DH], pb, over_rows, preferred_element_type=F32)
        dk = lax.dot_general(q_s[:, :DH], ds, over_rows, preferred_element_type=F32) * SCALE
        dq = lax.dot_general(ds, k, (((1,), (1,)), ((), ())), preferred_element_type=F32) * SCALE
        for n, i in enumerate(group):
            held[i, 0] = dk[:, n * cols : (n + 1) * cols]
            held[i, 1] = dv[:, n * cols : (n + 1) * cols]
            if not last:
                copies[i].start()
        if j == 0:
            acc[...] = dq
        else:
            acc[...] += dq

    if last:
        for b in range(blocks):
            dq_ref[b, 0] = near_ref[b]
    for b in range(blocks):
        out_ref = dq_ref.at[b, 1] if last else dq_ref.at[b]
        for h in range(HQ):
            at = pl.ds((h * blocks + b) * rows, rows)
            out_ref[:, h * DH : (h + 1) * DH] = acc[at, :].astype(BF)
    for j, copy in enumerate(copies):
        copy.wait()
        if last:
            total = held[j] + got[j]
            keep_ref[j] = total[:, :half]
            send_ref[j] = total[:, half:].astype(BF)


def grads(x, own, other, before=()):
    blocks = x.shape[0]
    rows = (x.shape[1] - STATS) // (2 * HQ)
    chunks, _, half, cols = own.shape
    total = blocks * rows * HQ
    last = len(before) > 0
    work = total * chunks * cols
    whole = pl.BlockSpec(memory_space=pltpu.VMEM)
    far = pl.BlockSpec(memory_space=pltpu.HBM)
    sums = (chunks, 2, 2 * half, cols)
    halves = (chunks, 2, half, cols)
    if last:
        operands = (x, own, other, *before)
        in_specs = [whole] * 4 + [far]
        out_shape = [
            jax.ShapeDtypeStruct((blocks, 2, rows, WIDTH), BF),
            jax.ShapeDtypeStruct(halves, F32),
            jax.ShapeDtypeStruct(halves, BF),
        ]
        out_specs = [whole] * 3
    else:
        operands = (x, own, other)
        in_specs = [whole] * 3
        out_shape = [
            jax.ShapeDtypeStruct((blocks, rows, WIDTH), BF),
            jax.ShapeDtypeStruct((SPARE * chunks,) + sums[1:], F32),
        ]
        out_specs = [whole, far]
    return pl.pallas_call(
        lambda *refs: grads_kernel(last, *refs),
        in_specs=in_specs,
        out_specs=out_specs,
        out_shape=out_shape,
        scratch_shapes=[
            pltpu.VMEM((total, 2 * DH), BF),
            pltpu.VMEM((total, 2 * DH), BF),
            pltpu.VMEM((total, DH), F32),
            pltpu.VMEM(sums, F32),
            pltpu.SemaphoreType.DMA((chunks,)),
        ]
        + [pltpu.VMEM(sums, F32)] * last,
        compiler_params=pltpu.CompilerParams(vmem_limit_bytes=VMEM_GRADS),
        cost_estimate=pl.CostEstimate(flops=10 * work * DH, bytes_accessed=4 << 20, transcendentals=work),
        name="grads",
    )(*operands)


def far_kernel(parts_ref, out_ref):
    total = parts_ref[0, 1].astype(F32)
    for b in range(1, parts_ref.shape[0]):
        total = total + parts_ref[b, 1].astype(F32)
    out_ref[...] = total.astype(BF)


def far_total(parts):
    return pl.pallas_call(
        far_kernel,
        out_shape=jax.ShapeDtypeStruct(parts.shape[2:], BF),
        compiler_params=SMALL,
        name="far_total",
    )(parts)


def query_kernel(core_ref, parts_ref, far_ref, out_ref):
    core = core_ref[0]
    for h in range(HQ):
        at = pl.ds(h * DH, DH)
        total = far_ref[:, at].astype(F32)
        for b in range(parts_ref.shape[0]):
            total = total + parts_ref[b, 0, :, at].astype(F32)
        out_ref[:, at] = half_swap(total, core).astype(BF)


def query_total(core, parts, far):
    return pl.pallas_call(
        query_kernel,
        in_specs=[pl.BlockSpec(memory_space=pltpu.SMEM)] + [pl.BlockSpec(memory_space=pltpu.VMEM)] * 2,
        out_shape=jax.ShapeDtypeStruct(far.shape, BF),
        compiler_params=SMALL,
        name="query_total",
    )(core, parts, far)


def both_kernel(y_ref, keep_ref, got_ref, *out_refs):
    count = len(out_refs)
    for r, out_ref in enumerate(out_refs):
        at = lax.rem(y_ref[0] + r, count)
        out_ref[...] = (keep_ref[at] + got_ref[at].astype(F32)).astype(out_ref.dtype)


def both_cores(y, keep, got):
    one = jax.ShapeDtypeStruct(keep.shape[1:], BF)
    return pl.pallas_call(
        both_kernel,
        in_specs=[pl.BlockSpec(memory_space=pltpu.SMEM)] + [pl.BlockSpec(memory_space=pltpu.VMEM)] * 2,
        out_shape=[one] * keep.shape[0],
        compiler_params=MEDIUM,
        name="both_cores",
    )(y, keep, got)


def visual_kernel(*refs):
    parts = refs[:-2]
    for i, out_ref in enumerate(refs[-2:]):
        total = parts[0][i].astype(F32)
        for part in parts[1:]:
            total = total + part[i].astype(F32)
        out_ref[...] = total.astype(BF)


def visual_total(parts):
    one = jax.ShapeDtypeStruct(parts[0].shape[1:], BF)
    return pl.pallas_call(
        visual_kernel, out_shape=[one, one], compiler_params=SMALL, name="visual_total"
    )(*parts)


def along(axis, value, steps):
    count = lax.axis_size(axis)
    return lax.ppermute(value, axis, [(i, (i + steps) % count) for i in range(count)])


def index(axis):
    return lax.axis_index(axis).astype(jnp.int32).reshape(1)


def per_device(queries, keys, values, outputs, out_grad, logsumexp):
    core = index("core")
    x, copies, kv = prep(core, queries, out_grad, outputs, logsumexp.T, keys, values)

    far = lax.ppermute(x, "zq", SWAP)
    x_near = lax.all_to_all(copies, "zi", 0, 0)

    own = lax.all_gather(kv, "y")
    far, own = lax.optimization_barrier((far, own))
    other = lax.ppermute(own, "core", SWAP)
    x_far = lax.all_to_all(jnp.broadcast_to(far, copies.shape), "zi", 0, 0)

    dq, keep, send = grads(x_far, own, other, grads(x_near, own, other))
    parts = lax.all_to_all(dq, "zi", 0, 0)
    query_grad = query_total(core, parts, lax.ppermute(far_total(parts), "zq", SWAP))

    both = both_cores(index("y"), keep, lax.ppermute(send, "core", SWAP))
    parts = [both[0]] + [along("y", both[r], r) for r in (1, 3, 2)]
    key_grad, value_grad = visual_total(parts)
    return query_grad, key_grad, value_grad


def solution(mesh):
    devices = mesh.devices.reshape(2, 4, 2, 4, 2, 4)
    inner = Mesh(devices, ("zh", "x", "core", "y", "zq", "zi"))
    head = ("zh", "x", "core")
    seq = ("y", "zq", "zi")
    text = P(seq, head)
    visual = P(head, seq)
    return jax.shard_map(
        per_device,
        mesh=inner,
        in_specs=(text, visual, visual, text, text, text),
        out_specs=(text, visual, visual),
        check_vma=False,
    )
```

```python
import jax
import jax.numpy as jnp
from jax import lax
from jax.experimental import pallas as pl
from jax.experimental.pallas import tpu as pltpu
from jax.sharding import Mesh, PartitionSpec as P

DH = 128
HQ = 4
WIDTH = HQ * DH
STATS = 4 * HQ
GROUP = 2
SCALE = DH**-0.5
LOG2E = 1.4426950408889634
BF = jnp.bfloat16
F32 = jnp.float32
SWAP = [(0, 1), (1, 0)]
VMEM_GRADS = 40 << 20
SPARE = 10
MEDIUM = pltpu.CompilerParams(vmem_limit_bytes=12 << 20)
SMALL = pltpu.CompilerParams(vmem_limit_bytes=4 << 20)


def half_swap(value, core):
    rolled = jnp.concatenate([value[:, DH // 2 :], value[:, : DH // 2]], 1)
    return jnp.where(core == 0, value, rolled)


def prep_kernel(core_ref, q_ref, g_ref, o_ref, lse_ref, k_ref, v_ref, x_ref, copies_ref, kv_ref):
    core = core_ref[0]
    rows = q_ref.shape[0]
    lane = lax.broadcasted_iota(jnp.int32, (rows, DH), 1)
    lse = jnp.transpose(lse_ref[...]) * (-1.0 / SCALE)
    stats = jnp.zeros((rows, DH), F32)
    for h in range(HQ):
        at = pl.ds(h * DH, DH)
        q = q_ref[:, at].astype(F32)
        g = g_ref[:, at].astype(F32)
        dterm = jnp.sum(g * o_ref[:, at].astype(F32), axis=1, keepdims=True)
        mine = (lane & (HQ - 1)) == h
        stats = jnp.where(mine & (lane < 2 * HQ), lse[:, h : h + 1], stats)
        stats = jnp.where(mine & (lane >= 2 * HQ) & (lane < STATS), -dterm, stats)
        x_ref[h * rows : (h + 1) * rows, :] = half_swap(q, core).astype(BF)
        x_ref[(HQ + h) * rows : (HQ + h + 1) * rows, :] = half_swap(g, core).astype(BF)
    high = stats.astype(BF).astype(F32)
    stats = jnp.where((lane & HQ) == 0, high, stats - high)
    stats = jnp.concatenate([stats, jnp.zeros((DH - rows, DH), F32)], 0)
    x_ref[2 * HQ * rows :, :] = jnp.transpose(stats)[:STATS].astype(BF)
    for b in range(copies_ref.shape[0]):
        copies_ref[b] = x_ref[...]
    kv_ref[0] = k_ref[...]
    kv_ref[1] = v_ref[...]


def prep(core, queries, out_grad, outputs, lse_t, keys, values):
    rows = queries.shape[0]
    return pl.pallas_call(
        prep_kernel,
        in_specs=[pl.BlockSpec(memory_space=pltpu.SMEM)] + [pl.BlockSpec(memory_space=pltpu.VMEM)] * 6,
        out_shape=[
            jax.ShapeDtypeStruct((2 * HQ * rows + STATS, DH), BF),
            jax.ShapeDtypeStruct((lax.axis_size("zi"), 2 * HQ * rows + STATS, DH), BF),
            jax.ShapeDtypeStruct((2,) + keys.shape, BF),
        ],
        name="prep",
    )(core, queries, out_grad, outputs, lse_t, keys, values)


def grads_kernel(last, *refs):
    if last:
        side_ref, x_ref, own_ref, other_ref, near_ref, before_ref, *refs = refs
        dq_ref, keep_ref, send_ref, q_s, g_s, acc, held, sems, got = refs
    else:
        x_ref, own_ref, other_ref, dq_ref, after_ref, q_s, g_s, acc, held, sems = refs
    blocks = x_ref.shape[0]
    rows = (x_ref.shape[1] - STATS) // (2 * HQ)
    chunks, _, half, cols = own_ref.shape
    copies = []
    for j in range(chunks):
        ends = (before_ref.at[j], got.at[j]) if last else (held.at[j], after_ref.at[j])
        copies.append(pltpu.make_async_copy(*ends, sems.at[j]))
        if last:
            copies[j].start()
    lane = lax.broadcasted_iota(jnp.int32, (rows, DH), 1)
    for b in range(blocks):
        stats = x_ref[b, 2 * HQ * rows :, :].astype(F32)
        stats = jnp.concatenate([stats, jnp.zeros((DH - STATS, DH), F32)], 0)
        stats = jnp.transpose(stats)[:rows]
        for h in range(HQ):
            to = pl.ds((h * blocks + b) * rows, rows)
            mine = jnp.where((lane & (HQ - 1)) == h, stats, 0.0).astype(BF)
            q_s[to, :DH] = x_ref[b, h * rows : (h + 1) * rows, :]
            g_s[to, :DH] = x_ref[b, (HQ + h) * rows : (HQ + h + 1) * rows, :]
            q_s[to, DH:] = mine
            g_s[to, DH:] = mine

    row = lax.broadcasted_iota(jnp.int32, (DH, GROUP * cols), 0)
    k_ones = jnp.where(row < STATS // 2, 1.0, 0.0).astype(BF)
    v_ones = jnp.where((row >= STATS // 2) & (row < STATS), 1.0, 0.0).astype(BF)
    over_rows = (((0,), (0,)), ((), ()))
    for j in range(0, chunks, GROUP):
        group = range(j, j + GROUP)
        k = jnp.concatenate([jnp.concatenate([own_ref[i, 0], other_ref[i, 0]], 0) for i in group], 1)
        v = jnp.concatenate([jnp.concatenate([own_ref[i, 1], other_ref[i, 1]], 0) for i in group], 1)
        s = jnp.dot(q_s[...], jnp.concatenate([k, k_ones], 0), preferred_element_type=F32)
        p = jnp.exp2(s * (SCALE * LOG2E))
        dp = jnp.dot(g_s[...], jnp.concatenate([v, v_ones], 0), preferred_element_type=F32)
        ds = (p * dp).astype(BF)
        pb = p.astype(BF)
        dv = lax.dot_general(g_s[:, :DH], pb, over_rows, preferred_element_type=F32)
        dk = lax.dot_general(q_s[:, :DH], ds, over_rows, preferred_element_type=F32) * SCALE
        dq = lax.dot_general(ds, k, (((1,), (1,)), ((), ())), preferred_element_type=F32) * SCALE
        for n, i in enumerate(group):
            held[i, 0] = dk[:, n * cols : (n + 1) * cols]
            held[i, 1] = dv[:, n * cols : (n + 1) * cols]
            if not last:
                copies[i].start()
        if j == 0:
            acc[...] = dq
        else:
            acc[...] += dq

    if last:
        side = side_ref[0]
        dq_ref[side] = near_ref[...]
    for b in range(blocks):
        out_ref = dq_ref.at[1 - side, b] if last else dq_ref.at[b]
        for h in range(HQ):
            at = pl.ds((h * blocks + b) * rows, rows)
            out_ref[:, h * DH : (h + 1) * DH] = acc[at, :].astype(BF)
    for j, copy in enumerate(copies):
        copy.wait()
        if last:
            total = held[j] + got[j]
            keep_ref[j] = total[:, :half]
            send_ref[j] = total[:, half:].astype(BF)


def grads(x, own, other, side=None, before=()):
    blocks = x.shape[0]
    rows = (x.shape[1] - STATS) // (2 * HQ)
    chunks, _, half, cols = own.shape
    total = blocks * rows * HQ
    last = side is not None
    work = total * chunks * cols
    small = pl.BlockSpec(memory_space=pltpu.SMEM)
    whole = pl.BlockSpec(memory_space=pltpu.VMEM)
    far = pl.BlockSpec(memory_space=pltpu.HBM)
    sums = (chunks, 2, 2 * half, cols)
    halves = (chunks, 2, half, cols)
    if last:
        operands = (side, x, own, other, *before)
        in_specs = [small] + [whole] * 4 + [far]
        out_shape = [
            jax.ShapeDtypeStruct((2, blocks, rows, WIDTH), BF),
            jax.ShapeDtypeStruct(halves, F32),
            jax.ShapeDtypeStruct(halves, BF),
        ]
        out_specs = [whole] * 3
    else:
        operands = (x, own, other)
        in_specs = [whole] * 3
        out_shape = [
            jax.ShapeDtypeStruct((blocks, rows, WIDTH), BF),
            jax.ShapeDtypeStruct((SPARE * chunks,) + sums[1:], F32),
        ]
        out_specs = [whole, far]
    return pl.pallas_call(
        lambda *refs: grads_kernel(last, *refs),
        in_specs=in_specs,
        out_specs=out_specs,
        out_shape=out_shape,
        scratch_shapes=[
            pltpu.VMEM((total, 2 * DH), BF),
            pltpu.VMEM((total, 2 * DH), BF),
            pltpu.VMEM((total, DH), F32),
            pltpu.VMEM(sums, F32),
            pltpu.SemaphoreType.DMA((chunks,)),
        ]
        + [pltpu.VMEM(sums, F32)] * last,
        compiler_params=pltpu.CompilerParams(vmem_limit_bytes=VMEM_GRADS),
        cost_estimate=pl.CostEstimate(flops=10 * work * DH, bytes_accessed=4 << 20, transcendentals=work),
        name="grads",
    )(*operands)


def query_kernel(core_ref, parts_ref, out_ref):
    core = core_ref[0]
    for h in range(HQ):
        at = pl.ds(h * DH, DH)
        total = parts_ref[0, :, at].astype(F32)
        for b in range(1, parts_ref.shape[0]):
            total = total + parts_ref[b, :, at].astype(F32)
        out_ref[:, at] = half_swap(total, core).astype(BF)


def query_total(core, parts):
    return pl.pallas_call(
        query_kernel,
        in_specs=[pl.BlockSpec(memory_space=pltpu.SMEM), pl.BlockSpec(memory_space=pltpu.VMEM)],
        out_shape=jax.ShapeDtypeStruct(parts.shape[1:], BF),
        compiler_params=SMALL,
        name="query_total",
    )(core, parts)


def both_kernel(y_ref, keep_ref, got_ref, *out_refs):
    count = len(out_refs)
    for r, out_ref in enumerate(out_refs):
        at = lax.rem(y_ref[0] + r, count)
        out_ref[...] = (keep_ref[at] + got_ref[at].astype(F32)).astype(out_ref.dtype)


def both_cores(y, keep, got):
    one = jax.ShapeDtypeStruct(keep.shape[1:], BF)
    return pl.pallas_call(
        both_kernel,
        in_specs=[pl.BlockSpec(memory_space=pltpu.SMEM)] + [pl.BlockSpec(memory_space=pltpu.VMEM)] * 2,
        out_shape=[one] * keep.shape[0],
        compiler_params=MEDIUM,
        name="both_cores",
    )(y, keep, got)


def visual_kernel(*refs):
    parts = refs[:-2]
    for i, out_ref in enumerate(refs[-2:]):
        total = parts[0][i].astype(F32)
        for part in parts[1:]:
            total = total + part[i].astype(F32)
        out_ref[...] = total.astype(BF)


def visual_total(parts):
    one = jax.ShapeDtypeStruct(parts[0].shape[1:], BF)
    return pl.pallas_call(
        visual_kernel, out_shape=[one, one], compiler_params=SMALL, name="visual_total"
    )(*parts)


def along(axis, value, steps):
    count = lax.axis_size(axis)
    return lax.ppermute(value, axis, [(i, (i + steps) % count) for i in range(count)])


def index(axis):
    return lax.axis_index(axis).astype(jnp.int32).reshape(1)


def per_device(queries, keys, values, outputs, out_grad, logsumexp):
    core = index("core")
    x, copies, kv = prep(core, queries, out_grad, outputs, logsumexp.T, keys, values)

    far = lax.ppermute(x, "zq", SWAP)
    x_near = lax.all_to_all(copies, "zi", 0, 0)

    own = lax.all_gather(kv, "y")
    far, own = lax.optimization_barrier((far, own))
    other = lax.ppermute(own, "core", SWAP)
    x_far = lax.all_to_all(jnp.broadcast_to(far, copies.shape), "zi", 0, 0)

    before = grads(x_near, own, other)
    dq, keep, send = grads(x_far, own, other, index("zq"), before)
    dq = dq.reshape((-1,) + dq.shape[2:])
    query_grad = query_total(core, lax.all_to_all(dq, ("zq", "zi"), 0, 0))

    both = both_cores(index("y"), keep, lax.ppermute(send, "core", SWAP))
    parts = [both[0]] + [along("y", both[r], r) for r in (1, 3, 2)]
    key_grad, value_grad = visual_total(parts)
    return query_grad, key_grad, value_grad


def solution(mesh):
    devices = mesh.devices.reshape(2, 4, 2, 4, 2, 4)
    inner = Mesh(devices, ("zh", "x", "core", "y", "zq", "zi"))
    head = ("zh", "x", "core")
    seq = ("y", "zq", "zi")
    text = P(seq, head)
    visual = P(head, seq)
    return jax.shard_map(
        per_device,
        mesh=inner,
        in_specs=(text, visual, visual, text, text, text),
        out_specs=(text, visual, visual),
        check_vma=False,
    )
```

```python
import jax
import jax.numpy as jnp
from jax import lax
from jax.experimental import pallas as pl
from jax.experimental.pallas import tpu as pltpu
from jax.sharding import Mesh, PartitionSpec as P

DH = 128
HQ = 4
WIDTH = HQ * DH
STATS = 4 * HQ
GROUP = 2
SCALE = DH**-0.5
LOG2E = 1.4426950408889634
BF = jnp.bfloat16
F32 = jnp.float32
SWAP = [(0, 1), (1, 0)]
VMEM_GRADS = 40 << 20
SPARE = 10
MEDIUM = pltpu.CompilerParams(vmem_limit_bytes=12 << 20)
SMALL = pltpu.CompilerParams(vmem_limit_bytes=4 << 20)


def half_swap(value, core):
    rolled = jnp.concatenate([value[:, DH // 2 :], value[:, : DH // 2]], 1)
    return jnp.where(core == 0, value, rolled)


def prep_kernel(core_ref, q_ref, g_ref, o_ref, lse_ref, k_ref, v_ref, x_ref, kv_ref):
    core = core_ref[0]
    rows = q_ref.shape[0]
    lane = lax.broadcasted_iota(jnp.int32, (rows, DH), 1)
    lse = jnp.transpose(lse_ref[...]) * (-1.0 / SCALE)
    stats = jnp.zeros((rows, DH), F32)
    for h in range(HQ):
        at = pl.ds(h * DH, DH)
        q = q_ref[:, at].astype(F32)
        g = g_ref[:, at].astype(F32)
        dterm = jnp.sum(g * o_ref[:, at].astype(F32), axis=1, keepdims=True)
        mine = (lane & (HQ - 1)) == h
        stats = jnp.where(mine & (lane < 2 * HQ), lse[:, h : h + 1], stats)
        stats = jnp.where(mine & (lane >= 2 * HQ) & (lane < STATS), -dterm, stats)
        x_ref[h * rows : (h + 1) * rows, :] = half_swap(q, core).astype(BF)
        x_ref[(HQ + h) * rows : (HQ + h + 1) * rows, :] = half_swap(g, core).astype(BF)
    high = stats.astype(BF).astype(F32)
    stats = jnp.where((lane & HQ) == 0, high, stats - high)
    stats = jnp.concatenate([stats, jnp.zeros((DH - rows, DH), F32)], 0)
    x_ref[2 * HQ * rows :, :] = jnp.transpose(stats)[:STATS].astype(BF)
    for y in range(kv_ref.shape[0]):
        kv_ref[y, 0] = k_ref[...]
        kv_ref[y, 1] = v_ref[...]


def prep(core, queries, out_grad, outputs, lse_t, keys, values):
    rows = queries.shape[0]
    return pl.pallas_call(
        prep_kernel,
        in_specs=[pl.BlockSpec(memory_space=pltpu.SMEM)] + [pl.BlockSpec(memory_space=pltpu.VMEM)] * 6,
        out_shape=[
            jax.ShapeDtypeStruct((2 * HQ * rows + STATS, DH), BF),
            jax.ShapeDtypeStruct((lax.axis_size("y"), 2) + keys.shape, BF),
        ],
        name="prep",
    )(core, queries, out_grad, outputs, lse_t, keys, values)


def grads_kernel(last, *refs):
    if last:
        side_ref, x_ref, own_ref, other_ref, near_ref, before_ref, *refs = refs
        dq_ref, keep_ref, send_ref, q_s, g_s, acc, held, sems, got = refs
    else:
        x_ref, own_ref, other_ref, dq_ref, after_ref, q_s, g_s, acc, held, sems = refs
    blocks = x_ref.shape[0]
    rows = (x_ref.shape[1] - STATS) // (2 * HQ)
    chunks, _, half, cols = own_ref.shape
    copies = []
    for j in range(chunks):
        ends = (before_ref.at[j], got.at[j]) if last else (held.at[j], after_ref.at[j])
        copies.append(pltpu.make_async_copy(*ends, sems.at[j]))
        if last:
            copies[j].start()
    lane = lax.broadcasted_iota(jnp.int32, (rows, DH), 1)
    for b in range(blocks):
        stats = x_ref[b, 2 * HQ * rows :, :].astype(F32)
        stats = jnp.concatenate([stats, jnp.zeros((DH - STATS, DH), F32)], 0)
        stats = jnp.transpose(stats)[:rows]
        for h in range(HQ):
            to = pl.ds((h * blocks + b) * rows, rows)
            mine = jnp.where((lane & (HQ - 1)) == h, stats, 0.0).astype(BF)
            q_s[to, :DH] = x_ref[b, h * rows : (h + 1) * rows, :]
            g_s[to, :DH] = x_ref[b, (HQ + h) * rows : (HQ + h + 1) * rows, :]
            q_s[to, DH:] = mine
            g_s[to, DH:] = mine

    row = lax.broadcasted_iota(jnp.int32, (DH, GROUP * cols), 0)
    k_ones = jnp.where(row < STATS // 2, 1.0, 0.0).astype(BF)
    v_ones = jnp.where((row >= STATS // 2) & (row < STATS), 1.0, 0.0).astype(BF)
    over_rows = (((0,), (0,)), ((), ()))
    for j in range(0, chunks, GROUP):
        group = range(j, j + GROUP)
        k = jnp.concatenate([jnp.concatenate([own_ref[i, 0], other_ref[i, 0]], 0) for i in group], 1)
        v = jnp.concatenate([jnp.concatenate([own_ref[i, 1], other_ref[i, 1]], 0) for i in group], 1)
        s = jnp.dot(q_s[...], jnp.concatenate([k, k_ones], 0), preferred_element_type=F32)
        p = jnp.exp2(s * (SCALE * LOG2E))
        dp = jnp.dot(g_s[...], jnp.concatenate([v, v_ones], 0), preferred_element_type=F32)
        ds = (p * dp).astype(BF)
        pb = p.astype(BF)
        dv = lax.dot_general(g_s[:, :DH], pb, over_rows, preferred_element_type=F32)
        dk = lax.dot_general(q_s[:, :DH], ds, over_rows, preferred_element_type=F32) * SCALE
        dq = lax.dot_general(ds, k, (((1,), (1,)), ((), ())), preferred_element_type=F32) * SCALE
        for n, i in enumerate(group):
            held[i, 0] = dk[:, n * cols : (n + 1) * cols]
            held[i, 1] = dv[:, n * cols : (n + 1) * cols]
            if not last:
                copies[i].start()
        if j == 0:
            acc[...] = dq
        else:
            acc[...] += dq

    if last:
        side = side_ref[0]
        dq_ref[side] = near_ref[...]
    for b in range(blocks):
        out_ref = dq_ref.at[1 - side, b] if last else dq_ref.at[b]
        for h in range(HQ):
            at = pl.ds((h * blocks + b) * rows, rows)
            out_ref[:, h * DH : (h + 1) * DH] = acc[at, :].astype(BF)
    for j, copy in enumerate(copies):
        copy.wait()
        if last:
            total = held[j] + got[j]
            keep_ref[j] = total[:, :half]
            send_ref[j] = total[:, half:].astype(BF)


def grads(x, own, other, side=None, before=()):
    blocks = x.shape[0]
    rows = (x.shape[1] - STATS) // (2 * HQ)
    chunks, _, half, cols = own.shape
    total = blocks * rows * HQ
    last = side is not None
    work = total * chunks * cols
    small = pl.BlockSpec(memory_space=pltpu.SMEM)
    whole = pl.BlockSpec(memory_space=pltpu.VMEM)
    far = pl.BlockSpec(memory_space=pltpu.HBM)
    sums = (chunks, 2, 2 * half, cols)
    halves = (chunks, 2, half, cols)
    if last:
        operands = (side, x, own, other, *before)
        in_specs = [small] + [whole] * 4 + [far]
        out_shape = [
            jax.ShapeDtypeStruct((2, blocks, rows, WIDTH), BF),
            jax.ShapeDtypeStruct(halves, F32),
            jax.ShapeDtypeStruct(halves, BF),
        ]
        out_specs = [whole] * 3
    else:
        operands = (x, own, other)
        in_specs = [whole] * 3
        out_shape = [
            jax.ShapeDtypeStruct((blocks, rows, WIDTH), BF),
            jax.ShapeDtypeStruct((SPARE * chunks,) + sums[1:], F32),
        ]
        out_specs = [whole, far]
    return pl.pallas_call(
        lambda *refs: grads_kernel(last, *refs),
        in_specs=in_specs,
        out_specs=out_specs,
        out_shape=out_shape,
        scratch_shapes=[
            pltpu.VMEM((total, 2 * DH), BF),
            pltpu.VMEM((total, 2 * DH), BF),
            pltpu.VMEM((total, DH), F32),
            pltpu.VMEM(sums, F32),
            pltpu.SemaphoreType.DMA((chunks,)),
        ]
        + [pltpu.VMEM(sums, F32)] * last,
        compiler_params=pltpu.CompilerParams(vmem_limit_bytes=VMEM_GRADS),
        cost_estimate=pl.CostEstimate(flops=10 * work * DH, bytes_accessed=4 << 20, transcendentals=work),
        name="grads",
    )(*operands)


def query_kernel(core_ref, parts_ref, out_ref):
    core = core_ref[0]
    for h in range(HQ):
        at = pl.ds(h * DH, DH)
        total = parts_ref[0, :, at].astype(F32)
        for b in range(1, parts_ref.shape[0]):
            total = total + parts_ref[b, :, at].astype(F32)
        out_ref[:, at] = half_swap(total, core).astype(BF)


def query_total(core, parts):
    return pl.pallas_call(
        query_kernel,
        in_specs=[pl.BlockSpec(memory_space=pltpu.SMEM), pl.BlockSpec(memory_space=pltpu.VMEM)],
        out_shape=jax.ShapeDtypeStruct(parts.shape[1:], BF),
        compiler_params=SMALL,
        name="query_total",
    )(core, parts)


def both_kernel(y_ref, keep_ref, got_ref, *out_refs):
    count = len(out_refs)
    for r, out_ref in enumerate(out_refs):
        at = lax.rem(y_ref[0] + r, count)
        out_ref[...] = (keep_ref[at] + got_ref[at].astype(F32)).astype(out_ref.dtype)


def both_cores(y, keep, got):
    one = jax.ShapeDtypeStruct(keep.shape[1:], BF)
    return pl.pallas_call(
        both_kernel,
        in_specs=[pl.BlockSpec(memory_space=pltpu.SMEM)] + [pl.BlockSpec(memory_space=pltpu.VMEM)] * 2,
        out_shape=[one] * keep.shape[0],
        compiler_params=MEDIUM,
        name="both_cores",
    )(y, keep, got)


def visual_kernel(*refs):
    parts = refs[:-2]
    for i, out_ref in enumerate(refs[-2:]):
        total = parts[0][i].astype(F32)
        for part in parts[1:]:
            total = total + part[i].astype(F32)
        out_ref[...] = total.astype(BF)


def visual_total(parts):
    one = jax.ShapeDtypeStruct(parts[0].shape[1:], BF)
    return pl.pallas_call(
        visual_kernel, out_shape=[one, one], compiler_params=SMALL, name="visual_total"
    )(*parts)


def along(axis, value, steps):
    count = lax.axis_size(axis)
    return lax.ppermute(value, axis, [(i, (i + steps) % count) for i in range(count)])


def index(axis):
    return lax.axis_index(axis).astype(jnp.int32).reshape(1)


def per_device(queries, keys, values, outputs, out_grad, logsumexp):
    core = index("core")
    x, kv = prep(core, queries, out_grad, outputs, logsumexp.T, keys, values)

    own = lax.all_to_all(kv, "y", 0, 0)
    far = lax.ppermute(x, "zq", SWAP)
    x_near = lax.all_gather(x, "zi")
    far, x_near, own = lax.optimization_barrier((far, x_near, own))
    other = lax.ppermute(own, "core", SWAP)
    x_far = lax.all_to_all(jnp.broadcast_to(far, x_near.shape), "zi", 0, 0)

    before = grads(x_near, own, other)
    dq, keep, send = grads(x_far, own, other, index("zq"), before)
    dq = dq.reshape((-1,) + dq.shape[2:])
    query_grad = query_total(core, lax.all_to_all(dq, ("zq", "zi"), 0, 0))

    both = both_cores(index("y"), keep, lax.ppermute(send, "core", SWAP))
    parts = [both[0]] + [along("y", both[r], r) for r in (1, 3, 2)]
    key_grad, value_grad = visual_total(parts)
    return query_grad, key_grad, value_grad


def solution(mesh):
    devices = mesh.devices.reshape(2, 4, 2, 4, 2, 4)
    inner = Mesh(devices, ("zh", "x", "core", "y", "zq", "zi"))
    head = ("zh", "x", "core")
    seq = ("y", "zq", "zi")
    text = P(seq, head)
    visual = P(head, seq)
    return jax.shard_map(
        per_device,
        mesh=inner,
        in_specs=(text, visual, visual, text, text, text),
        out_specs=(text, visual, visual),
        check_vma=False,
    )
```

```python
import jax
import jax.numpy as jnp
from jax import lax
from jax.experimental import pallas as pl
from jax.experimental.pallas import tpu as pltpu
from jax.sharding import Mesh, PartitionSpec as P

DH = 128
HQ = 4
WIDTH = HQ * DH
STATS = 4 * HQ
GROUP = 2
SCALE = DH**-0.5
LOG2E = 1.4426950408889634
BF = jnp.bfloat16
F32 = jnp.float32
SWAP = [(0, 1), (1, 0)]
VMEM_GRADS = 40 << 20
SPARE = 10
MEDIUM = pltpu.CompilerParams(vmem_limit_bytes=12 << 20)
SMALL = pltpu.CompilerParams(vmem_limit_bytes=4 << 20)


def half_swap(value, core):
    rolled = jnp.concatenate([value[:, DH // 2 :], value[:, : DH // 2]], 1)
    return jnp.where(core == 0, value, rolled)


def prep_kernel(core_ref, q_ref, g_ref, o_ref, lse_ref, k_ref, v_ref, x_ref, copies_ref, kv_ref):
    core = core_ref[0]
    rows = q_ref.shape[0]
    lane = lax.broadcasted_iota(jnp.int32, (rows, DH), 1)
    lse = jnp.transpose(lse_ref[...]) * (-1.0 / SCALE)
    stats = jnp.zeros((rows, DH), F32)
    for h in range(HQ):
        at = pl.ds(h * DH, DH)
        q = q_ref[:, at].astype(F32)
        g = g_ref[:, at].astype(F32)
        dterm = jnp.sum(g * o_ref[:, at].astype(F32), axis=1, keepdims=True)
        mine = (lane & (HQ - 1)) == h
        stats = jnp.where(mine & (lane < 2 * HQ), lse[:, h : h + 1], stats)
        stats = jnp.where(mine & (lane >= 2 * HQ) & (lane < STATS), -dterm, stats)
        x_ref[h * rows : (h + 1) * rows, :] = half_swap(q, core).astype(BF)
        x_ref[(HQ + h) * rows : (HQ + h + 1) * rows, :] = half_swap(g, core).astype(BF)
    high = stats.astype(BF).astype(F32)
    stats = jnp.where((lane & HQ) == 0, high, stats - high)
    stats = jnp.concatenate([stats, jnp.zeros((DH - rows, DH), F32)], 0)
    x_ref[2 * HQ * rows :, :] = jnp.transpose(stats)[:STATS].astype(BF)
    for b in range(copies_ref.shape[0]):
        copies_ref[b] = x_ref[...]
    kv_ref[0] = k_ref[...]
    kv_ref[1] = v_ref[...]


def prep(core, queries, out_grad, outputs, lse_t, keys, values):
    rows = queries.shape[0]
    return pl.pallas_call(
        prep_kernel,
        in_specs=[pl.BlockSpec(memory_space=pltpu.SMEM)] + [pl.BlockSpec(memory_space=pltpu.VMEM)] * 6,
        out_shape=[
            jax.ShapeDtypeStruct((2 * HQ * rows + STATS, DH), BF),
            jax.ShapeDtypeStruct((lax.axis_size("zi"), 2 * HQ * rows + STATS, DH), BF),
            jax.ShapeDtypeStruct((2,) + keys.shape, BF),
        ],
        name="prep",
    )(core, queries, out_grad, outputs, lse_t, keys, values)


def copies_kernel(x_ref, out_ref, sems):
    copies = [pltpu.make_async_copy(x_ref, out_ref.at[b], sems.at[b]) for b in range(out_ref.shape[0])]
    for copy in copies:
        copy.start()
    for copy in copies:
        copy.wait()


def copies_of(x, count):
    return pl.pallas_call(
        copies_kernel,
        in_specs=[pl.BlockSpec(memory_space=pltpu.VMEM)],
        out_specs=pl.BlockSpec(memory_space=pltpu.HBM),
        out_shape=jax.ShapeDtypeStruct((count,) + x.shape, x.dtype),
        scratch_shapes=[pltpu.SemaphoreType.DMA((count,))],
        compiler_params=SMALL,
        name="copies_of",
    )(x)


def grads_kernel(last, *refs):
    if last:
        side_ref, x_ref, own_ref, other_ref, near_ref, before_ref, *refs = refs
        dq_ref, keep_ref, send_ref, q_s, g_s, acc, held, sems, got = refs
    else:
        x_ref, own_ref, other_ref, dq_ref, after_ref, q_s, g_s, acc, held, sems = refs
    blocks = x_ref.shape[0]
    rows = (x_ref.shape[1] - STATS) // (2 * HQ)
    chunks, _, half, cols = own_ref.shape
    copies = []
    for j in range(chunks):
        ends = (before_ref.at[j], got.at[j]) if last else (held.at[j], after_ref.at[j])
        copies.append(pltpu.make_async_copy(*ends, sems.at[j]))
        if last:
            copies[j].start()
    lane = lax.broadcasted_iota(jnp.int32, (rows, DH), 1)
    for b in range(blocks):
        stats = x_ref[b, 2 * HQ * rows :, :].astype(F32)
        stats = jnp.concatenate([stats, jnp.zeros((DH - STATS, DH), F32)], 0)
        stats = jnp.transpose(stats)[:rows]
        for h in range(HQ):
            to = pl.ds((h * blocks + b) * rows, rows)
            mine = jnp.where((lane & (HQ - 1)) == h, stats, 0.0).astype(BF)
            q_s[to, :DH] = x_ref[b, h * rows : (h + 1) * rows, :]
            g_s[to, :DH] = x_ref[b, (HQ + h) * rows : (HQ + h + 1) * rows, :]
            q_s[to, DH:] = mine
            g_s[to, DH:] = mine

    row = lax.broadcasted_iota(jnp.int32, (DH, GROUP * cols), 0)
    k_ones = jnp.where(row < STATS // 2, 1.0, 0.0).astype(BF)
    v_ones = jnp.where((row >= STATS // 2) & (row < STATS), 1.0, 0.0).astype(BF)
    over_rows = (((0,), (0,)), ((), ()))
    for j in range(0, chunks, GROUP):
        group = range(j, j + GROUP)
        k = jnp.concatenate([jnp.concatenate([own_ref[i, 0], other_ref[i, 0]], 0) for i in group], 1)
        v = jnp.concatenate([jnp.concatenate([own_ref[i, 1], other_ref[i, 1]], 0) for i in group], 1)
        s = jnp.dot(q_s[...], jnp.concatenate([k, k_ones], 0), preferred_element_type=F32)
        p = jnp.exp2(s * (SCALE * LOG2E))
        dp = jnp.dot(g_s[...], jnp.concatenate([v, v_ones], 0), preferred_element_type=F32)
        ds = (p * dp).astype(BF)
        pb = p.astype(BF)
        dv = lax.dot_general(g_s[:, :DH], pb, over_rows, preferred_element_type=F32)
        dk = lax.dot_general(q_s[:, :DH], ds, over_rows, preferred_element_type=F32) * SCALE
        dq = lax.dot_general(ds, k, (((1,), (1,)), ((), ())), preferred_element_type=F32) * SCALE
        for n, i in enumerate(group):
            held[i, 0] = dk[:, n * cols : (n + 1) * cols]
            held[i, 1] = dv[:, n * cols : (n + 1) * cols]
            if not last:
                copies[i].start()
        if j == 0:
            acc[...] = dq
        else:
            acc[...] += dq

    if last:
        side = side_ref[0]
        dq_ref[side] = near_ref[...]
    for b in range(blocks):
        out_ref = dq_ref.at[1 - side, b] if last else dq_ref.at[b]
        for h in range(HQ):
            at = pl.ds((h * blocks + b) * rows, rows)
            out_ref[:, h * DH : (h + 1) * DH] = acc[at, :].astype(BF)
    for j, copy in enumerate(copies):
        copy.wait()
        if last:
            total = held[j] + got[j]
            keep_ref[j] = total[:, :half].astype(BF)
            send_ref[j] = total[:, half:].astype(BF)


def grads(x, own, other, side=None, before=()):
    blocks = x.shape[0]
    rows = (x.shape[1] - STATS) // (2 * HQ)
    chunks, _, half, cols = own.shape
    total = blocks * rows * HQ
    last = side is not None
    work = total * chunks * cols
    small = pl.BlockSpec(memory_space=pltpu.SMEM)
    whole = pl.BlockSpec(memory_space=pltpu.VMEM)
    far = pl.BlockSpec(memory_space=pltpu.HBM)
    sums = (chunks, 2, 2 * half, cols)
    halves = (chunks, 2, half, cols)
    if last:
        operands = (side, x, own, other, *before)
        in_specs = [small] + [whole] * 4 + [far]
        out_shape = [
            jax.ShapeDtypeStruct((2, blocks, rows, WIDTH), BF),
            jax.ShapeDtypeStruct(halves, BF),
            jax.ShapeDtypeStruct(halves, BF),
        ]
        out_specs = [whole] * 3
    else:
        operands = (x, own, other)
        in_specs = [whole] * 3
        out_shape = [
            jax.ShapeDtypeStruct((blocks, rows, WIDTH), BF),
            jax.ShapeDtypeStruct((SPARE * chunks,) + sums[1:], F32),
        ]
        out_specs = [whole, far]
    return pl.pallas_call(
        lambda *refs: grads_kernel(last, *refs),
        in_specs=in_specs,
        out_specs=out_specs,
        out_shape=out_shape,
        scratch_shapes=[
            pltpu.VMEM((total, 2 * DH), BF),
            pltpu.VMEM((total, 2 * DH), BF),
            pltpu.VMEM((total, DH), F32),
            pltpu.VMEM(sums, F32),
            pltpu.SemaphoreType.DMA((chunks,)),
        ]
        + [pltpu.VMEM(sums, F32)] * last,
        compiler_params=pltpu.CompilerParams(vmem_limit_bytes=VMEM_GRADS),
        cost_estimate=pl.CostEstimate(flops=10 * work * DH, bytes_accessed=4 << 20, transcendentals=work),
        name="grads",
    )(*operands)


def query_kernel(core_ref, parts_ref, out_ref):
    core = core_ref[0]
    for h in range(HQ):
        at = pl.ds(h * DH, DH)
        total = parts_ref[0, :, at].astype(F32)
        for b in range(1, parts_ref.shape[0]):
            total = total + parts_ref[b, :, at].astype(F32)
        out_ref[:, at] = half_swap(total, core).astype(BF)


def query_total(core, parts):
    return pl.pallas_call(
        query_kernel,
        in_specs=[pl.BlockSpec(memory_space=pltpu.SMEM), pl.BlockSpec(memory_space=pltpu.VMEM)],
        out_shape=jax.ShapeDtypeStruct(parts.shape[1:], BF),
        compiler_params=SMALL,
        name="query_total",
    )(core, parts)


def both_kernel(y_ref, keep_ref, got_ref, *out_refs):
    count = len(out_refs)
    for r, out_ref in enumerate(out_refs):
        at = lax.rem(y_ref[0] + r, count)
        out_ref[...] = (keep_ref[at].astype(F32) + got_ref[at].astype(F32)).astype(out_ref.dtype)


def both_cores(y, keep, got):
    one = jax.ShapeDtypeStruct(keep.shape[1:], BF)
    return pl.pallas_call(
        both_kernel,
        in_specs=[pl.BlockSpec(memory_space=pltpu.SMEM)] + [pl.BlockSpec(memory_space=pltpu.VMEM)] * 2,
        out_shape=[one] * keep.shape[0],
        compiler_params=MEDIUM,
        name="both_cores",
    )(y, keep, got)


def visual_kernel(*refs):
    parts = refs[:-2]
    for i, out_ref in enumerate(refs[-2:]):
        total = parts[0][i].astype(F32)
        for part in parts[1:]:
            total = total + part[i].astype(F32)
        out_ref[...] = total.astype(BF)


def visual_total(parts):
    one = jax.ShapeDtypeStruct(parts[0].shape[1:], BF)
    return pl.pallas_call(
        visual_kernel, out_shape=[one, one], compiler_params=SMALL, name="visual_total"
    )(*parts)


def along(axis, value, steps):
    count = lax.axis_size(axis)
    return lax.ppermute(value, axis, [(i, (i + steps) % count) for i in range(count)])


def index(axis):
    return lax.axis_index(axis).astype(jnp.int32).reshape(1)


def per_device(queries, keys, values, outputs, out_grad, logsumexp):
    core = index("core")
    x, copies, kv = prep(core, queries, out_grad, outputs, logsumexp.T, keys, values)

    far = lax.ppermute(x, "zq", SWAP)
    x_near = lax.all_to_all(copies, "zi", 0, 0)

    own = lax.all_gather(kv, "y")
    far, own = lax.optimization_barrier((far, own))
    other = lax.ppermute(own, "core", SWAP)
    x_far = lax.all_to_all(copies_of(far, copies.shape[0]), "zi", 0, 0)

    before = grads(x_near, own, other)
    dq, keep, send = grads(x_far, own, other, index("zq"), before)
    dq = dq.reshape((-1,) + dq.shape[2:])
    query_grad = query_total(core, lax.all_to_all(dq, ("zq", "zi"), 0, 0))

    both = both_cores(index("y"), keep, lax.ppermute(send, "core", SWAP))
    parts = [both[0]] + [along("y", both[r], r) for r in (1, 3, 2)]
    key_grad, value_grad = visual_total(parts)
    return query_grad, key_grad, value_grad


def solution(mesh):
    devices = mesh.devices.reshape(2, 4, 2, 4, 2, 4)
    inner = Mesh(devices, ("zh", "x", "core", "y", "zq", "zi"))
    head = ("zh", "x", "core")
    seq = ("y", "zq", "zi")
    text = P(seq, head)
    visual = P(head, seq)
    return jax.shard_map(
        per_device,
        mesh=inner,
        in_specs=(text, visual, visual, text, text, text),
        out_specs=(text, visual, visual),
        check_vma=False,
    )
```

```python
import jax
import jax.numpy as jnp
from jax import lax
from jax.experimental import pallas as pl
from jax.experimental.pallas import tpu as pltpu
from jax.sharding import Mesh, PartitionSpec as P

DH = 128
HQ = 4
WIDTH = HQ * DH
STATS = 4 * HQ
GROUP = 2
SCALE = DH**-0.5
LOG2E = 1.4426950408889634
BF = jnp.bfloat16
F32 = jnp.float32
SWAP = [(0, 1), (1, 0)]
VMEM_GRADS = 40 << 20
SPARE = 10
MEDIUM = pltpu.CompilerParams(vmem_limit_bytes=12 << 20)
SMALL = pltpu.CompilerParams(vmem_limit_bytes=4 << 20)


def half_swap(value, core):
    rolled = jnp.concatenate([value[:, DH // 2 :], value[:, : DH // 2]], 1)
    return jnp.where(core == 0, value, rolled)


def prep_kernel(core_ref, q_ref, g_ref, o_ref, lse_ref, k_ref, v_ref, x_ref, copies_ref, kv_ref):
    core = core_ref[0]
    rows = q_ref.shape[0]
    lane = lax.broadcasted_iota(jnp.int32, (rows, DH), 1)
    lse = jnp.transpose(lse_ref[...]) * (-1.0 / SCALE)
    stats = jnp.zeros((rows, DH), F32)
    for h in range(HQ):
        at = pl.ds(h * DH, DH)
        q = q_ref[:, at].astype(F32)
        g = g_ref[:, at].astype(F32)
        dterm = jnp.sum(g * o_ref[:, at].astype(F32), axis=1, keepdims=True)
        mine = (lane & (HQ - 1)) == h
        stats = jnp.where(mine & (lane < 2 * HQ), lse[:, h : h + 1], stats)
        stats = jnp.where(mine & (lane >= 2 * HQ) & (lane < STATS), -dterm, stats)
        x_ref[h * rows : (h + 1) * rows, :] = half_swap(q, core).astype(BF)
        x_ref[(HQ + h) * rows : (HQ + h + 1) * rows, :] = half_swap(g, core).astype(BF)
    high = stats.astype(BF).astype(F32)
    stats = jnp.where((lane & HQ) == 0, high, stats - high)
    stats = jnp.concatenate([stats, jnp.zeros((DH - rows, DH), F32)], 0)
    x_ref[2 * HQ * rows :, :] = jnp.transpose(stats)[:STATS].astype(BF)
    for b in range(copies_ref.shape[0]):
        copies_ref[b] = x_ref[...]
    kv_ref[0] = k_ref[...]
    kv_ref[1] = v_ref[...]


def prep(core, queries, out_grad, outputs, lse_t, keys, values):
    rows = queries.shape[0]
    return pl.pallas_call(
        prep_kernel,
        in_specs=[pl.BlockSpec(memory_space=pltpu.SMEM)] + [pl.BlockSpec(memory_space=pltpu.VMEM)] * 6,
        out_shape=[
            jax.ShapeDtypeStruct((2 * HQ * rows + STATS, DH), BF),
            jax.ShapeDtypeStruct((lax.axis_size("zi"), 2 * HQ * rows + STATS, DH), BF),
            jax.ShapeDtypeStruct((2,) + keys.shape, BF),
        ],
        name="prep",
    )(core, queries, out_grad, outputs, lse_t, keys, values)


def copies_kernel(x_ref, out_ref, sems):
    copies = [pltpu.make_async_copy(x_ref, out_ref.at[b], sems.at[b]) for b in range(out_ref.shape[0])]
    for copy in copies:
        copy.start()
    for copy in copies:
        copy.wait()


def copies_of(x, count):
    return pl.pallas_call(
        copies_kernel,
        in_specs=[pl.BlockSpec(memory_space=pltpu.VMEM)],
        out_specs=pl.BlockSpec(memory_space=pltpu.HBM),
        out_shape=jax.ShapeDtypeStruct((count,) + x.shape, x.dtype),
        scratch_shapes=[pltpu.SemaphoreType.DMA((count,))],
        compiler_params=SMALL,
        name="copies_of",
    )(x)


def grads_kernel(last, *refs):
    if last:
        side_ref, x_ref, own_ref, other_ref, near_ref, before_ref, *refs = refs
        dq_ref, keep_ref, send_ref, q_s, g_s, acc, held, sems, got = refs
    else:
        x_ref, own_ref, other_ref, dq_ref, after_ref, q_s, g_s, acc, held, sems = refs
    blocks = x_ref.shape[0]
    rows = (x_ref.shape[1] - STATS) // (2 * HQ)
    chunks, _, half, cols = own_ref.shape
    copies = []
    for j in range(chunks):
        ends = (before_ref.at[j], got.at[j]) if last else (held.at[j], after_ref.at[j])
        copies.append(pltpu.make_async_copy(*ends, sems.at[j]))
        if last:
            copies[j].start()
    lane = lax.broadcasted_iota(jnp.int32, (rows, DH), 1)
    for b in range(blocks):
        stats = x_ref[b, 2 * HQ * rows :, :].astype(F32)
        stats = jnp.concatenate([stats, jnp.zeros((DH - STATS, DH), F32)], 0)
        stats = jnp.transpose(stats)[:rows]
        for h in range(HQ):
            to = pl.ds((h * blocks + b) * rows, rows)
            mine = jnp.where((lane & (HQ - 1)) == h, stats, 0.0).astype(BF)
            q_s[to, :DH] = x_ref[b, h * rows : (h + 1) * rows, :]
            g_s[to, :DH] = x_ref[b, (HQ + h) * rows : (HQ + h + 1) * rows, :]
            q_s[to, DH:] = mine
            g_s[to, DH:] = mine

    row = lax.broadcasted_iota(jnp.int32, (DH, GROUP * cols), 0)
    k_ones = jnp.where(row < STATS // 2, 1.0, 0.0).astype(BF)
    v_ones = jnp.where((row >= STATS // 2) & (row < STATS), 1.0, 0.0).astype(BF)
    over_rows = (((0,), (0,)), ((), ()))
    for j in range(0, chunks, GROUP):
        group = range(j, j + GROUP)
        k = jnp.concatenate([jnp.concatenate([own_ref[i, 0], other_ref[i, 0]], 0) for i in group], 1)
        v = jnp.concatenate([jnp.concatenate([own_ref[i, 1], other_ref[i, 1]], 0) for i in group], 1)
        s = jnp.dot(q_s[...], jnp.concatenate([k, k_ones], 0), preferred_element_type=F32)
        p = jnp.exp2(s * (SCALE * LOG2E))
        dp = jnp.dot(g_s[...], jnp.concatenate([v, v_ones], 0), preferred_element_type=F32)
        ds = (p * dp).astype(BF)
        pb = p.astype(BF)
        dv = lax.dot_general(g_s[:, :DH], pb, over_rows, preferred_element_type=F32)
        dk = lax.dot_general(q_s[:, :DH], ds, over_rows, preferred_element_type=F32) * SCALE
        dq = lax.dot_general(ds, k, (((1,), (1,)), ((), ())), preferred_element_type=F32) * SCALE
        for n, i in enumerate(group):
            held[i, 0] = dk[:, n * cols : (n + 1) * cols]
            held[i, 1] = dv[:, n * cols : (n + 1) * cols]
            if not last:
                copies[i].start()
        if j == 0:
            acc[...] = dq
        else:
            acc[...] += dq

    if last:
        side = side_ref[0]
        dq_ref[side] = near_ref[...]
    for b in range(blocks):
        out_ref = dq_ref.at[1 - side, b] if last else dq_ref.at[b]
        for h in range(HQ):
            at = pl.ds((h * blocks + b) * rows, rows)
            out_ref[:, h * DH : (h + 1) * DH] = acc[at, :].astype(BF)
    for j, copy in enumerate(copies):
        copy.wait()
        if last:
            total = held[j] + got[j]
            keep_ref[j] = total[:, :half].astype(BF)
            send_ref[j] = total[:, half:].astype(BF)


def grads(x, own, other, side=None, before=()):
    blocks = x.shape[0]
    rows = (x.shape[1] - STATS) // (2 * HQ)
    chunks, _, half, cols = own.shape
    total = blocks * rows * HQ
    last = side is not None
    work = total * chunks * cols
    small = pl.BlockSpec(memory_space=pltpu.SMEM)
    whole = pl.BlockSpec(memory_space=pltpu.VMEM)
    far = pl.BlockSpec(memory_space=pltpu.HBM)
    sums = (chunks, 2, 2 * half, cols)
    halves = (chunks, 2, half, cols)
    if last:
        operands = (side, x, own, other, *before)
        in_specs = [small] + [whole] * 4 + [far]
        out_shape = [
            jax.ShapeDtypeStruct((2, blocks, rows, WIDTH), BF),
            jax.ShapeDtypeStruct(halves, BF),
            jax.ShapeDtypeStruct(halves, BF),
        ]
        out_specs = [whole] * 3
    else:
        operands = (x, own, other)
        in_specs = [whole] * 3
        out_shape = [
            jax.ShapeDtypeStruct((blocks, rows, WIDTH), BF),
            jax.ShapeDtypeStruct((SPARE * chunks,) + sums[1:], F32),
        ]
        out_specs = [whole, far]
    return pl.pallas_call(
        lambda *refs: grads_kernel(last, *refs),
        in_specs=in_specs,
        out_specs=out_specs,
        out_shape=out_shape,
        scratch_shapes=[
            pltpu.VMEM((total, 2 * DH), BF),
            pltpu.VMEM((total, 2 * DH), BF),
            pltpu.VMEM((total, DH), F32),
            pltpu.VMEM(sums, F32),
            pltpu.SemaphoreType.DMA((chunks,)),
        ]
        + [pltpu.VMEM(sums, F32)] * last,
        compiler_params=pltpu.CompilerParams(vmem_limit_bytes=VMEM_GRADS),
        cost_estimate=pl.CostEstimate(flops=10 * work * DH, bytes_accessed=4 << 20, transcendentals=work),
        name="grads",
    )(*operands)


def query_kernel(core_ref, parts_ref, out_ref):
    core = core_ref[0]
    for h in range(HQ):
        at = pl.ds(h * DH, DH)
        total = parts_ref[0, :, at].astype(F32)
        for b in range(1, parts_ref.shape[0]):
            total = total + parts_ref[b, :, at].astype(F32)
        out_ref[:, at] = half_swap(total, core).astype(BF)


def query_total(core, parts):
    return pl.pallas_call(
        query_kernel,
        in_specs=[pl.BlockSpec(memory_space=pltpu.SMEM), pl.BlockSpec(memory_space=pltpu.VMEM)],
        out_shape=jax.ShapeDtypeStruct(parts.shape[1:], BF),
        compiler_params=SMALL,
        name="query_total",
    )(core, parts)


def both_kernel(y_ref, keep_ref, got_ref, *out_refs):
    count = len(out_refs)
    for r, out_ref in enumerate(out_refs):
        at = lax.rem(y_ref[0] + r, count)
        out_ref[...] = (keep_ref[at].astype(F32) + got_ref[at].astype(F32)).astype(out_ref.dtype)


def both_cores(y, keep, got):
    one = jax.ShapeDtypeStruct(keep.shape[1:], BF)
    return pl.pallas_call(
        both_kernel,
        in_specs=[pl.BlockSpec(memory_space=pltpu.SMEM)] + [pl.BlockSpec(memory_space=pltpu.VMEM)] * 2,
        out_shape=[one] * keep.shape[0],
        compiler_params=MEDIUM,
        name="both_cores",
    )(y, keep, got)


def visual_kernel(*refs):
    parts = refs[:-2]
    for i, out_ref in enumerate(refs[-2:]):
        total = parts[0][i].astype(F32)
        for part in parts[1:]:
            total = total + part[i].astype(F32)
        out_ref[...] = total.astype(BF)


def visual_total(parts):
    one = jax.ShapeDtypeStruct(parts[0].shape[1:], BF)
    return pl.pallas_call(
        visual_kernel, out_shape=[one, one], compiler_params=SMALL, name="visual_total"
    )(*parts)


def along(axis, value, steps):
    count = lax.axis_size(axis)
    return lax.ppermute(value, axis, [(i, (i + steps) % count) for i in range(count)])


def index(axis):
    return lax.axis_index(axis).astype(jnp.int32).reshape(1)


def per_device(queries, keys, values, outputs, out_grad, logsumexp):
    core = index("core")
    x, copies, kv = prep(core, queries, out_grad, outputs, logsumexp.T, keys, values)

    far = lax.ppermute(x, "zq", SWAP)
    x_near = lax.all_to_all(copies, "zi", 0, 0)

    own = lax.all_gather(kv, "y")
    far, own = lax.optimization_barrier((far, own))
    other = lax.ppermute(own, "core", SWAP)
    x_far = lax.all_to_all(copies_of(far, copies.shape[0]), "zi", 0, 0)

    before = grads(x_near, own, other)
    dq, keep, send = grads(x_far, own, other, index("zq"), before)
    dq = dq.reshape((-1,) + dq.shape[2:])
    query_grad = query_total(core, lax.all_to_all(dq, ("zq", "zi"), 0, 0))

    both = both_cores(index("y"), keep, lax.ppermute(send, "core", SWAP))
    parts = [both[0]] + [along("y", both[r], r) for r in (2, 1, 3)]
    key_grad, value_grad = visual_total(parts)
    return query_grad, key_grad, value_grad


def solution(mesh):
    devices = mesh.devices.reshape(2, 4, 2, 4, 2, 4)
    inner = Mesh(devices, ("zh", "x", "core", "y", "zq", "zi"))
    head = ("zh", "x", "core")
    seq = ("y", "zq", "zi")
    text = P(seq, head)
    visual = P(head, seq)
    return jax.shard_map(
        per_device,
        mesh=inner,
        in_specs=(text, visual, visual, text, text, text),
        out_specs=(text, visual, visual),
        check_vma=False,
    )
```
